32 devices in a mesh: blk: 16 (over z, y, core), rows: 2 (over x).
Axes of the slice: x: 2, y: 2, z: 4, core: 2. Of those that a mesh axis runs over, the one named last changes fastest.
Arguments:
- q_panel: bfloat16 [2, 512, 256], P('rows', 'blk'), may hold values from -6 to 6
- tiles: bfloat16 [16, 2, 20, 128, 128], P('blk', 'rows'), may hold values from -0.15625 to 0.15625
- tile_rows: int32 [16, 2, 20], P('blk', 'rows'), may hold values from 0 to 3
- tile_cols: int32 [16, 2, 20, 1], P('blk', 'rows'), may hold values from 0 to 3; in each aligned block of 20 rows (0 to 19, 20 to 39, ..., all dimensions but the last counted through in order) at most 7 rows name the same one
- tile_count: int32 [16, 2], P('blk', 'rows'), may hold values from 10 to 20, as said below
- owner_map: int32 [16, 4], P('blk'), may hold values from 0 to 3, each once within a row
Outputs:
- y_basis: bfloat16 [16, 512, 256], P('blk', 'rows')
- z_basis: float32 [2, 512, 256], P('rows', 'blk')
The draws below stay inside these ranges and needn't reach their ends.
Inputs may be any that keep to these rules, and one draw needn't show every extreme that they name: The live tiles of a device are its first tile_count slots; some device has all 20 live and some has 10. `tile_cols`: among the 20 slots of one device no column block appears more than 7 times. Each row of owner_map is a permutation; slot s belongs to the device with rows index s // 2.
All inputs are finite; a program needn't handle non-finite values.
Results may differ from the reference program's by a relative error of at most 0.0013.
Values may be sent and summed in bfloat16 or wider, within the bound.
No kernel may reach another device: no remote copies, remote signals or barrier semaphores. Data moves between devices by JAX's collectives and lax.ppermute only.
A program may use at most 64 MiB of HBM per device.

```python
import math
import jax
import jax.numpy as jnp
import numpy as np
from jax import lax

TILE = 128
RANK = 256
TPB = 5
RB_DEV = 2
MOST = 7
NCB = 4
TILES_DEV = 20
RBG = 4
N_BLK = 16
N_ROWS = 2


def draw_tile_count(key, part):
    counts = jax.random.randint(key, (N_BLK * N_ROWS,), TILES_DEV // 2, TILES_DEV + 1)
    picked = jax.random.permutation(jax.random.fold_in(key, 7), N_BLK * N_ROWS)
    counts = counts.at[picked[0]].set(TILES_DEV).at[picked[1]].set(TILES_DEV // 2)
    return counts.reshape(N_BLK, N_ROWS).astype(jnp.int32)


def with_ends(entries, stream_key, low, largest):
    shape = entries.shape
    spot = [jax.random.randint(jax.random.fold_in(stream_key, axis), (), 0, shape[axis]) for axis in range(len(shape))]
    entries = entries.at[tuple(spot)].set(low)
    longest = shape.index(max(shape))
    spot[longest] = (spot[longest] + 1) % shape[longest]
    return entries.at[tuple(spot)].set(largest)


def block_levels(stream_key, dims, split, smallest, top_value):
    factor_of = 1.0
    for position, parts in split:
        draws = jax.random.uniform(jax.random.fold_in(jax.random.fold_in(stream_key, 6), position), (parts,), jnp.float32, smallest / len(split), top_value / len(split))
        factor_of = factor_of * jnp.repeat(jnp.exp(draws), dims[position] // parts).reshape((-1,) + (1,) * (len(dims) - 1 - position))
    return factor_of


def deal_out(rng, own, number, rows, number_of, top, bound, lean):
    order = jax.random.permutation(rng, number_of)
    heavy_load, usual = portions_of(number_of, rows * top, bound, lean, True), portions_of(number_of, rows * top, bound, lean, False)
    places = jnp.arange(number_of)

    def named(lengths, turn):
        used = int((lengths > 0).sum())
        fixed = max(1, used // 4)
        moved = fixed + (places - fixed + turn * (used - fixed)) % max(1, number_of - fixed)
        return jnp.zeros((number_of,), jnp.int32).at[order[jnp.where(places < fixed, places, moved)]].set(jnp.asarray(lengths, jnp.int32))

    lengths = jnp.where(number % 4 == 0, named(heavy_load, number // 4), named(usual, number - number // 4 - 1))
    mixed = jax.random.permutation(jax.random.fold_in(own, 3), number_of)
    donor, receiver = mixed[0:number_of // 2 * 2:2], mixed[1:number_of // 2 * 2:2]
    room = jnp.minimum(lengths[donor] - 1, bound - lengths[receiver]) // 2
    room = jnp.where((donor == order[0]) | (receiver == order[0]) | (lengths[receiver] == 0), 0, jnp.maximum(room, 0))
    moved = jax.random.randint(jax.random.fold_in(own, 4), (number_of // 2,), 0, 1 << 20) % (room + 1)
    lengths = lengths.at[donor].add(-moved).at[receiver].add(moved)
    items = jnp.searchsorted(jnp.cumsum(lengths), jnp.arange(rows * top), side="right").astype(jnp.int32)
    listing = items.reshape(top, rows).T
    listing = listing[jax.random.permutation(jax.random.fold_in(own, 1), rows)]
    turn = jax.random.randint(jax.random.fold_in(own, 2), (rows, 1), 0, top)
    return jnp.take_along_axis(listing, (jnp.arange(top)[None, :] + turn) % top, axis=1)


def portions_of(amount, total, most, lean, full):
    portions = [(1 << 20) // math.isqrt(standing ** lean) + 1 for standing in range(1, amount + 1)]
    largest = most if full else min(most, max(-(-total // amount), total * portions[0] // sum(portions)))
    least = 1 if total - largest >= amount - 1 else 0
    given, rest = [largest] + [least] * (amount - 1), total - largest - least * (amount - 1)
    while rest > 0:
        candidates = [i for i in range(1, amount) if given[i] < largest] or [i for i in range(1, amount) if given[i] < most]
        whole, left = sum([portions[i] for i in candidates]), rest
        for i in candidates:
            addition = min(most - given[i], max(1, left * portions[i] // whole), rest)
            given[i] = given[i] + addition
            rest = rest - addition
    return np.array(given)


def gaussian(own_key, shape, spread, bound, cuts=(), kind=jnp.bfloat16):
    result = jax.random.normal(own_key, shape, jnp.float32) * spread
    if len(cuts) > 0:
        result = block_levels(own_key, shape, cuts, -0.22, 0.18) * result
    return jnp.clip(result, min=-bound, max=bound).astype(kind)


def setup_inputs(seed: int = 0) -> dict:
    streams_of = jax.random.split(jax.random.key(seed), 7)
    q_panel = gaussian(streams_of[0], (N_ROWS, NCB * TILE, RANK), 1.0, 6.0, ((0, 2), (1, 16)))
    tiles = gaussian(streams_of[1], (N_BLK, N_ROWS, TILES_DEV, TILE, TILE), (TPB * NCB * TILE // RB_DEV) ** -0.5, 0.15625, ((0, 16), (1, 2)))
    tile_rows = with_ends(jax.random.randint(streams_of[2], (N_BLK, N_ROWS, TILES_DEV), 0, RBG), jax.random.fold_in(streams_of[2], 1), 0, RBG - 1).astype(jnp.int32)
    tile_cols_keys = jax.random.split(jax.random.fold_in(streams_of[3], 1), N_BLK * N_ROWS * TILES_DEV // TILES_DEV)
    tile_cols_turns = jax.random.permutation(jax.random.fold_in(streams_of[3], 3), N_BLK * N_ROWS * TILES_DEV // TILES_DEV)
    tile_cols = jax.vmap(lambda own, number: deal_out(jax.random.fold_in(streams_of[3], 2), own, number, TILES_DEV, NCB, 1, MOST, 2))(tile_cols_keys, tile_cols_turns).reshape((N_BLK, N_ROWS, TILES_DEV, 1))
    tile_count = draw_tile_count(jax.random.fold_in(streams_of[6], 71), 0)
    owner_map = jax.vmap(lambda own: jax.random.permutation(own, RBG))(jax.random.split(streams_of[5], N_BLK)).reshape((N_BLK, RBG)).astype(jnp.int32)
    return {"q_panel": q_panel, "tiles": tiles, "tile_rows": tile_rows, "tile_cols": tile_cols, "tile_count": tile_count, "owner_map": owner_map}


def reference(q_panel, tiles, tile_rows, tile_cols, tile_count, owner_map):
    q_blocks = q_panel.reshape(N_ROWS, NCB, TILE, RANK)
    active = (jnp.arange(TILES_DEV, dtype=jnp.int32)[None, None, :] < tile_count[:, :, None]).astype(jnp.float32)
    column_ids = tile_cols[..., 0]
    class_index = jnp.arange(N_ROWS, dtype=jnp.int32)[:, None]

    def forward(group):
        chosen = q_blocks[class_index, column_ids[group]]
        product = jnp.einsum("rtij,rtjk->rtik", tiles[group].astype(jnp.float32), chosen.astype(jnp.float32), precision=lax.Precision.HIGHEST)
        product = product * active[group][:, :, None, None]
        return jnp.zeros((RBG, TILE, RANK), jnp.float32).at[tile_rows[group]].add(product)

    y_full = lax.map(forward, jnp.arange(N_BLK, dtype=jnp.int32)).astype(jnp.bfloat16)
    group_index = jnp.arange(N_BLK, dtype=jnp.int32)[:, None]
    y_slots = jnp.zeros((N_BLK, RBG, TILE, RANK), jnp.bfloat16).at[group_index, owner_map].set(y_full)
    y_basis = y_slots.reshape(N_BLK, RBG * TILE, RANK)

    def backward(running, group):
        chosen = y_full[group][tile_rows[group]]
        product = jnp.einsum("rtji,rtjk->rtik", tiles[group].astype(jnp.float32), chosen.astype(jnp.float32), precision=lax.Precision.HIGHEST)
        product = product * active[group][:, :, None, None]
        return running.at[class_index, column_ids[group]].add(product), None

    start_sum = jnp.zeros((N_ROWS, NCB, TILE, RANK), jnp.float32)
    z_blocks, _ = lax.scan(backward, start_sum, jnp.arange(N_BLK, dtype=jnp.int32))
    return y_basis, z_blocks.reshape(N_ROWS, NCB * TILE, RANK)
```

```python
import jax
import jax.numpy as jnp
from jax import lax
from jax.experimental import pallas as pl
from jax.experimental.pallas import tpu as pltpu
from jax.sharding import PartitionSpec as P


def sides_of(chips):
    sides = ([], [])
    load = [0, 0]
    for k in sorted(range(chips), key=lambda k: -(k // 2 + k % 2)):
        open_sides = [c for c in range(2) if len(sides[c]) < chips // 2]
        c = min(open_sides, key=lambda c: load[c])
        sides[c].append(k)
        load[c] += k // 2 + k % 2
    return sides


def block_kernel(rounds, sides, *refs):
    direct, relayed = refs[:rounds], refs[rounds : 2 * rounds]
    (own_tiles, far_tiles, own_rows, own_cols, own_count, owners, far_meta) = refs[
        2 * rounds : 2 * rounds + 7
    ]
    outs = refs[2 * rounds + 7 :]
    y_out, keep, give = outs[0], outs[1 : 1 + rounds], outs[1 + rounds : 1 + 2 * rounds]
    near, far, own_a, far_a, y_all, z_all = outs[1 + 2 * rounds :]
    total, size = own_tiles.shape[0], own_tiles.shape[1]
    group = owners.shape[1]
    shard = direct[0].shape[0] // 4
    place = lax.axis_index("blk")
    core, chip = lax.rem(place, 2), lax.div(place, 2)
    half = lax.axis_index("rows")

    def rows_of(which, side):
        return pl.ds(pl.multiple_of(which * (2 * shard) + side * shard, shard), shard)

    def chip_of(step, side):
        return lax.bitwise_xor(chip, jnp.where(side == 0, sides[0][step], sides[1][step]))

    for step in range(rounds):
        for ref, side, first in (
            (direct[step], core, core),
            (relayed[step], 1 - core, 1 - core),
        ):
            which = chip_of(step, side)
            near[rows_of(which, first), :] = ref[0:shard, :]
            far[rows_of(which, first), :] = ref[shard : 2 * shard, :]
            near[rows_of(which, 1 - first), :] = ref[2 * shard : 3 * shard, :]
            far[rows_of(which, 1 - first), :] = ref[3 * shard : 4 * shard, :]

    def place_tiles(a, tiles, row_at, col_at, count):
        a[...] = jnp.zeros_like(a)

        def add(t, carry):
            rows = pl.ds(pl.multiple_of(row_at(t) * size, size), size)
            cols = pl.ds(pl.multiple_of(col_at(t) * size, size), size)
            a[rows, cols] = a[rows, cols] + tiles[t].astype(jnp.float32)
            return carry

        lax.fori_loop(0, count, add, 0)
        high = a[...].astype(jnp.bfloat16)
        low = (a[...] - high.astype(jnp.float32)).astype(jnp.bfloat16)
        return high, low

    own_high, own_low = place_tiles(
        own_a, own_tiles, lambda t: own_rows[0, 0, t], lambda t: own_cols[0, t], own_count[0, 0]
    )
    far_high, far_low = place_tiles(
        far_a,
        far_tiles,
        lambda t: far_meta[0, t],
        lambda t: far_meta[0, total + t],
        far_meta[0, 2 * total],
    )

    def dot(a, b):
        return jnp.dot(a, b, preferred_element_type=jnp.float32)

    q_near, q_far = near[...], far[...]
    y = (dot(own_high, q_near) + dot(far_high, q_far)) + (
        dot(own_low, q_near) + dot(far_low, q_far)
    )
    y16 = y.astype(jnp.bfloat16)
    y_all[...] = y16
    mine = group // 2
    for k in range(group):
        slot = owners[0, k]

        @pl.when(lax.div(slot, mine) == half)
        def _():
            at = pl.multiple_of(lax.rem(slot, mine) * size, size)
            y_out[pl.ds(at, size), :] = y_all[k * size : (k + 1) * size, :]

    def turned(a, b):
        return lax.dot_general(
            a, b, (((0,), (0,)), ((), ())), preferred_element_type=jnp.float32
        )

    z_all[...] = turned(own_high, y16) + turned(own_low, y16)
    for step in range(rounds):
        for ref, side, first in (
            (keep[step], core, core),
            (give[step], 1 - core, 1 - core),
        ):
            which = chip_of(step, side)
            ref[0:shard, :] = z_all[rows_of(which, first), :]
            ref[shard : 2 * shard, :] = z_all[rows_of(which, 1 - first), :]


def paired(q_panel, tiles, tile_rows, tile_cols, tile_count, owner_map):
    devices = lax.axis_size("blk")
    chips = devices // 2
    rounds = chips // 2
    sides = sides_of(chips)
    shard, rank = q_panel.shape[1:]
    stack = tiles[0, 0]
    total, size = stack.shape[:2]
    group = owner_map.shape[1]
    cols = tile_cols.reshape(1, total)

    across = [(0, 1), (1, 0)]
    sibling = [(i, i ^ 1) for i in range(devices)]

    def to_chips(step):
        return [
            (2 * m + c, 2 * (m ^ sides[c][step]) + c)
            for m in range(chips)
            for c in range(2)
        ]

    order = tuple(range(rounds))

    q_own = q_panel[0]
    q_far = lax.ppermute(q_own, "rows", across)
    stack, q_far = lax.optimization_barrier((stack, q_far))
    far_tiles = lax.ppermute(stack, "rows", across)
    meta = jnp.concatenate(
        [tile_rows.reshape(1, total), cols, tile_count.reshape(1, 1)], axis=1
    )
    far_meta = lax.ppermute(meta, "rows", across)
    pair = jnp.concatenate([q_own, q_far], axis=0)
    block = jnp.concatenate([pair, lax.ppermute(pair, "blk", sibling)], axis=0)
    direct, relayed = [None] * rounds, [None] * rounds
    for step in order:
        direct[step] = lax.ppermute(block, "blk", to_chips(step))
    for step in order:
        relayed[step] = lax.ppermute(direct[step], "blk", sibling)

    vmem = pl.BlockSpec(memory_space=pltpu.VMEM)
    smem = pl.BlockSpec(memory_space=pltpu.SMEM)
    width = devices * shard
    height = group * size
    piece = jax.ShapeDtypeStruct((2 * shard, rank), jnp.float32)

    def body(*refs):
        block_kernel(rounds, sides, *refs)

    made = pl.pallas_call(
        body,
        out_shape=[jax.ShapeDtypeStruct((height // 2, rank), jnp.bfloat16)]
        + [piece] * (2 * rounds),
        in_specs=[vmem] * (2 * rounds + 2) + [smem] * 5,
        out_specs=[vmem] * (1 + 2 * rounds),
        scratch_shapes=[
            pltpu.VMEM((width, rank), jnp.bfloat16),
            pltpu.VMEM((width, rank), jnp.bfloat16),
            pltpu.VMEM((height, width), jnp.float32),
            pltpu.VMEM((height, width), jnp.float32),
            pltpu.VMEM((height, rank), jnp.bfloat16),
            pltpu.VMEM((width, rank), jnp.float32),
        ],
        compiler_params=pltpu.CompilerParams(vmem_limit_bytes=24 << 20),
        name="block_products",
    )(*direct, *relayed, stack, far_tiles, tile_rows, cols, tile_count, owner_map, far_meta)
    y_owned, keep, give = made[0], made[1 : 1 + rounds], made[1 + rounds :]
    came = [None] * rounds
    for step in order:
        came[step] = lax.ppermute(give[step], "blk", sibling)
    arrived = [None] * rounds
    for step in order:
        arrived[step] = lax.ppermute(keep[step] + came[step], "blk", to_chips(step))
    summed = arrived[0]
    for step in range(1, rounds):
        summed = summed + arrived[step]
    z_share = summed[:shard] + lax.ppermute(summed[shard:], "blk", sibling)
    return (y_owned[None], z_share[None])


def general(q_panel, tiles, tile_rows, tile_cols, tile_count, owner_map):
    panel_rows = q_panel.shape[1]
    tile_stack = tiles[0, 0]
    tile_total = tile_stack.shape[0]
    tile_size = tile_stack.shape[1]
    group_blocks = owner_map.shape[1]
    class_blocks = panel_rows * lax.axis_size("blk") // tile_size
    column_ids = tile_cols[0, 0, :, 0]
    active = jnp.arange(tile_total, dtype=jnp.int32) < tile_count[0, 0]
    slot_of_tile = owner_map[0][tile_rows[0, 0]]
    slot_hit = slot_of_tile[:, None] == jnp.arange(group_blocks, dtype=jnp.int32)[None, :]
    column_hit = column_ids[:, None] == jnp.arange(class_blocks, dtype=jnp.int32)[None, :]
    placing = (slot_hit[:, :, None] & column_hit[:, None, :] & active[:, None, None]).astype(
        tile_stack.dtype
    )
    local_matrix = jnp.einsum(
        "tsc,tik->sick", placing, tile_stack, preferred_element_type=jnp.float32
    )
    local_matrix = local_matrix.reshape(group_blocks * tile_size, class_blocks * tile_size)
    rows_in = lax.all_gather(q_panel, "blk", axis=1, tiled=True)[0]
    flat_partial = jnp.dot(
        local_matrix, rows_in.astype(jnp.float32), precision=lax.Precision.HIGHEST
    )
    owned = lax.psum_scatter(flat_partial, "rows", scatter_dimension=0, tiled=True)
    y_owned = owned.astype(jnp.bfloat16)
    y_group = lax.all_gather(y_owned, "rows", axis=0, tiled=True)
    column_term = lax.dot_general(
        local_matrix,
        y_group.astype(jnp.float32),
        (((0,), (0,)), ((), ())),
        precision=lax.Precision.HIGHEST,
    )
    z_share = lax.psum_scatter(column_term, "blk", scatter_dimension=0, tiled=True)
    return (y_owned[None], z_share[None])


def solution(mesh):
    placed = (
        P("rows", "blk", None),
        P("blk", "rows", None, None, None),
        P("blk", "rows", None),
        P("blk", "rows", None, None),
        P("blk", "rows"),
        P("blk", None),
    )
    devices = mesh.shape["blk"]
    fits = mesh.shape["rows"] == 2 and devices >= 4 and devices & (devices - 1) == 0
    return jax.shard_map(
        paired if fits else general,
        mesh=mesh,
        in_specs=placed,
        out_specs=(P("blk", "rows", None), P("rows", "blk", None)),
        check_vma=False,
    )
```

```python
import jax
import jax.numpy as jnp
from jax import lax
from jax.experimental import pallas as pl
from jax.experimental.pallas import tpu as pltpu
from jax.sharding import PartitionSpec as P

NOTES, LANES = 16, 128


def sides_of(chips):
    sides = ([], [])
    load = [0, 0]
    for k in sorted(range(chips), key=lambda k: -(k // 2 + k % 2)):
        open_sides = [c for c in range(2) if len(sides[c]) < chips // 2]
        c = min(open_sides, key=lambda c: load[c])
        sides[c].append(k)
        load[c] += k // 2 + k % 2
    return sides


def parcel_kernel(tiles_hbm, rows_hbm, cols_hbm, count_hbm, owners_hbm, parcel, notes, *scratch):
    rows, cols, count, owners, sems = scratch
    height = tiles_hbm.shape[0]
    copies = [
        pltpu.make_async_copy(source, target, sems.at[i])
        for i, (source, target) in enumerate(
            (
                (rows_hbm, rows),
                (cols_hbm, cols),
                (count_hbm, count),
                (owners_hbm, owners),
                (tiles_hbm, parcel.at[0:height, :]),
            )
        )
    ]
    for copy in copies:
        copy.start()
    notes[...] = jnp.zeros_like(notes)
    for copy in copies[:4]:
        copy.wait()
    notes[0:1, 0 : rows.shape[1]] = rows[...]
    notes[1:2, 0 : cols.shape[1]] = cols[...]
    notes[2:3, 0:1] = count[...]
    notes[3:4, 0 : owners.shape[1]] = owners[...]
    parcel[height:, :] = notes[...].astype(jnp.float32).astype(parcel.dtype)
    copies[4].wait()


def block_kernel(rounds, sides, *refs):
    direct, relayed = refs[:rounds][::-1], refs[rounds : 2 * rounds][::-1]
    own_notes, own_parcel, far_parcel = refs[2 * rounds : 2 * rounds + 3]
    outs = refs[2 * rounds + 3 :]
    y_out, keep, give = outs[0], outs[1 : 1 + rounds], outs[1 + rounds : 1 + 2 * rounds]
    near, far, own_a, far_a, y_all, z_all, far_notes, scalars, sems = outs[1 + 2 * rounds :]
    size = own_parcel.shape[1]
    height = own_parcel.shape[0] - NOTES
    shard = direct[0].shape[0] // 4
    group = own_a.shape[0] // size
    place = lax.axis_index("blk")
    core, chip = lax.rem(place, 2), lax.div(place, 2)
    half = lax.axis_index("rows")

    far_notes[...] = far_parcel[height:, :].astype(jnp.float32).astype(jnp.int32)
    tells = [
        pltpu.make_async_copy(own_notes, scalars.at[0], sems.at[0]),
        pltpu.make_async_copy(far_notes, scalars.at[1], sems.at[1]),
    ]
    for tell in tells:
        tell.start()

    def rows_of(which, side):
        return pl.ds(pl.multiple_of(which * (2 * shard) + side * shard, shard), shard)

    def chip_of(step, side):
        return lax.bitwise_xor(chip, jnp.where(side == 0, sides[0][step], sides[1][step]))

    for step in range(rounds):
        for ref, side in ((direct[step], core), (relayed[step], 1 - core)):
            which = chip_of(step, side)
            near[rows_of(which, side), :] = ref[0:shard, :]
            far[rows_of(which, side), :] = ref[shard : 2 * shard, :]
            near[rows_of(which, 1 - side), :] = ref[2 * shard : 3 * shard, :]
            far[rows_of(which, 1 - side), :] = ref[3 * shard : 4 * shard, :]

    def place_tiles(a, tiles, at):
        a[...] = jnp.zeros_like(a)

        def add(t, carry):
            rows = pl.ds(pl.multiple_of(scalars[at, 0, t] * size, size), size)
            cols = pl.ds(pl.multiple_of(scalars[at, 1, t] * size, size), size)
            a[rows, cols] = a[rows, cols] + tiles[pl.ds(pl.multiple_of(t * size, size), size), :].astype(jnp.float32)
            return carry

        lax.fori_loop(0, scalars[at, 2, 0], add, 0)
        high = a[...].astype(jnp.bfloat16)
        low = (a[...] - high.astype(jnp.float32)).astype(jnp.bfloat16)
        return high, low

    for tell in tells:
        tell.wait()
    own_high, own_low = place_tiles(own_a, own_parcel, 0)
    far_high, far_low = place_tiles(far_a, far_parcel, 1)

    def dot(a, b):
        return jnp.dot(a, b, preferred_element_type=jnp.float32)

    q_near, q_far = near[...], far[...]
    y = (dot(own_high, q_near) + dot(far_high, q_far)) + (
        dot(own_low, q_near) + dot(far_low, q_far)
    )
    y16 = y.astype(jnp.bfloat16)
    y_all[...] = y16
    mine = group // 2
    for k in range(group):
        slot = scalars[0, 3, k]

        @pl.when(lax.div(slot, mine) == half)
        def _():
            at = pl.multiple_of(lax.rem(slot, mine) * size, size)
            y_out[pl.ds(at, size), :] = y_all[k * size : (k + 1) * size, :]

    def turned(a, b):
        return lax.dot_general(
            a, b, (((0,), (0,)), ((), ())), preferred_element_type=jnp.float32
        )

    z_all[...] = turned(own_high, y16) + turned(own_low, y16)
    for step in range(rounds):
        for ref, side in ((keep[step], core), (give[step], 1 - core)):
            which = chip_of(step, side)
            ref[0:shard, :] = z_all[rows_of(which, side), :]
            ref[shard : 2 * shard, :] = z_all[rows_of(which, 1 - side), :]


def paired(q_panel, tiles, tile_rows, tile_cols, tile_count, owner_map):
    devices = lax.axis_size("blk")
    chips = devices // 2
    rounds = chips // 2
    sides = sides_of(chips)
    shard, rank = q_panel.shape[1:]
    stack = tiles[0, 0]
    total, size = stack.shape[:2]
    group = owner_map.shape[1]

    across = [(0, 1), (1, 0)]
    sibling = [(i, i ^ 1) for i in range(devices)]

    def to_chips(step):
        return [
            (2 * m + c, 2 * (m ^ sides[c][step]) + c)
            for m in range(chips)
            for c in range(2)
        ]

    order = tuple(range(rounds))
    vmem = pl.BlockSpec(memory_space=pltpu.VMEM)

    q_own = q_panel[0]
    q_far = lax.ppermute(q_own, "rows", across)
    q_sibling = lax.ppermute(q_own, "blk", sibling)
    parcel, notes = pl.pallas_call(
        parcel_kernel,
        out_shape=[
            jax.ShapeDtypeStruct((total * size + NOTES, size), stack.dtype),
            jax.ShapeDtypeStruct((NOTES, LANES), jnp.int32),
        ],
        in_specs=[pl.BlockSpec(memory_space=pl.ANY)] * 5,
        out_specs=[vmem] * 2,
        scratch_shapes=[
            pltpu.VMEM((1, total), jnp.int32),
            pltpu.VMEM((1, total), jnp.int32),
            pltpu.VMEM((1, 1), jnp.int32),
            pltpu.VMEM((1, group), jnp.int32),
            pltpu.SemaphoreType.DMA((5,)),
        ],
        compiler_params=pltpu.CompilerParams(vmem_limit_bytes=24 << 20),
        name="parcel",
    )(
        stack.reshape(total * size, size),
        tile_rows.reshape(1, total),
        tile_cols.reshape(1, total),
        tile_count,
        owner_map,
    )
    late_parcel, q_far = lax.optimization_barrier((parcel, q_far))
    far_parcel = lax.ppermute(late_parcel, "rows", across)
    q_diagonal = lax.ppermute(q_far, "blk", sibling)
    block = jnp.concatenate([q_own, q_far, q_sibling, q_diagonal], axis=0)
    direct, relayed = [None] * rounds, [None] * rounds
    for step in reversed(order):
        direct[step] = lax.ppermute(block, "blk", to_chips(step))
    for step in reversed(order):
        relayed[step] = lax.ppermute(direct[step], "blk", sibling)

    width = devices * shard
    height = group * size
    piece = jax.ShapeDtypeStruct((2 * shard, rank), jnp.float32)

    def body(*refs):
        block_kernel(rounds, sides, *refs)

    made = pl.pallas_call(
        body,
        out_shape=[jax.ShapeDtypeStruct((height // 2, rank), jnp.bfloat16)]
        + [piece] * (2 * rounds),
        in_specs=[vmem] * (2 * rounds + 3),
        out_specs=[vmem] * (1 + 2 * rounds),
        scratch_shapes=[
            pltpu.VMEM((width, rank), jnp.bfloat16),
            pltpu.VMEM((width, rank), jnp.bfloat16),
            pltpu.VMEM((height, width), jnp.float32),
            pltpu.VMEM((height, width), jnp.float32),
            pltpu.VMEM((height, rank), jnp.bfloat16),
            pltpu.VMEM((width, rank), jnp.float32),
            pltpu.VMEM((NOTES, LANES), jnp.int32),
            pltpu.SMEM((2, NOTES, LANES), jnp.int32),
            pltpu.SemaphoreType.DMA((2,)),
        ],
        compiler_params=pltpu.CompilerParams(vmem_limit_bytes=24 << 20),
        name="block_products",
    )(*direct[::-1], *relayed[::-1], notes, parcel, far_parcel)
    y_owned, keep, give = made[0], made[1 : 1 + rounds], made[1 + rounds :]
    came = [None] * rounds
    for step in order:
        came[step] = lax.ppermute(give[step], "blk", sibling)
    arrived = [None] * rounds
    for step in order:
        arrived[step] = lax.ppermute(keep[step] + came[step], "blk", to_chips(step))
    summed = arrived[0]
    for step in range(1, rounds):
        summed = summed + arrived[step]
    z_share = summed[:shard] + lax.ppermute(summed[shard:], "blk", sibling)
    return (y_owned[None], z_share[None])


def general(q_panel, tiles, tile_rows, tile_cols, tile_count, owner_map):
    panel_rows = q_panel.shape[1]
    tile_stack = tiles[0, 0]
    tile_total = tile_stack.shape[0]
    tile_size = tile_stack.shape[1]
    group_blocks = owner_map.shape[1]
    class_blocks = panel_rows * lax.axis_size("blk") // tile_size
    column_ids = tile_cols[0, 0, :, 0]
    active = jnp.arange(tile_total, dtype=jnp.int32) < tile_count[0, 0]
    slot_of_tile = owner_map[0][tile_rows[0, 0]]
    slot_hit = slot_of_tile[:, None] == jnp.arange(group_blocks, dtype=jnp.int32)[None, :]
    column_hit = column_ids[:, None] == jnp.arange(class_blocks, dtype=jnp.int32)[None, :]
    placing = (slot_hit[:, :, None] & column_hit[:, None, :] & active[:, None, None]).astype(
        tile_stack.dtype
    )
    local_matrix = jnp.einsum(
        "tsc,tik->sick", placing, tile_stack, preferred_element_type=jnp.float32
    )
    local_matrix = local_matrix.reshape(group_blocks * tile_size, class_blocks * tile_size)
    rows_in = lax.all_gather(q_panel, "blk", axis=1, tiled=True)[0]
    flat_partial = jnp.dot(
        local_matrix, rows_in.astype(jnp.float32), precision=lax.Precision.HIGHEST
    )
    owned = lax.psum_scatter(flat_partial, "rows", scatter_dimension=0, tiled=True)
    y_owned = owned.astype(jnp.bfloat16)
    y_group = lax.all_gather(y_owned, "rows", axis=0, tiled=True)
    column_term = lax.dot_general(
        local_matrix,
        y_group.astype(jnp.float32),
        (((0,), (0,)), ((), ())),
        precision=lax.Precision.HIGHEST,
    )
    z_share = lax.psum_scatter(column_term, "blk", scatter_dimension=0, tiled=True)
    return (y_owned[None], z_share[None])


def solution(mesh):
    placed = (
        P("rows", "blk", None),
        P("blk", "rows", None, None, None),
        P("blk", "rows", None),
        P("blk", "rows", None, None),
        P("blk", "rows"),
        P("blk", None),
    )
    devices = mesh.shape["blk"]
    fits = mesh.shape["rows"] == 2 and devices >= 4 and devices & (devices - 1) == 0
    return jax.shard_map(
        paired if fits else general,
        mesh=mesh,
        in_specs=placed,
        out_specs=(P("blk", "rows", None), P("rows", "blk", None)),
        check_vma=False,
    )
```

```python
import jax
import jax.numpy as jnp
from jax import lax
from jax.experimental import pallas as pl
from jax.experimental.pallas import tpu as pltpu
from jax.sharding import PartitionSpec as P


LANES = 128
SCALE_ROWS = 16
VMEM_BYTES = 24 << 20


def sides_of(chips):
    sides = ([], [])
    load = [0, 0]
    for k in sorted(range(chips), key=lambda k: -(k // 2 + k % 2)):
        open_sides = [c for c in range(2) if len(sides[c]) < chips // 2]
        c = min(open_sides, key=lambda c: load[c])
        sides[c].append(k)
        load[c] += k // 2 + k % 2
    return sides


def own_place(sides, shard):
    place = lax.axis_index("blk")
    core, chip = lax.rem(place, 2), lax.div(place, 2)

    def rows_of(step, side, owner):
        which = lax.bitwise_xor(chip, jnp.where(side == 0, sides[0][step], sides[1][step]))
        return pl.ds(pl.multiple_of(which * (2 * shard) + owner * shard, shard), shard)

    return core, rows_of


def coded(x):
    top = jnp.max(jnp.abs(x), axis=0, keepdims=True)
    power = jnp.ceil(jnp.log2(jnp.maximum(top, 1e-30)))
    whole = jnp.round(x * jnp.exp2(15.0 - power))
    whole = jnp.clip(whole, -32767.0, 32767.0)
    return whole.astype(jnp.int32).astype(jnp.int16), power


def decoded(whole, power):
    return whole.astype(jnp.int32).astype(jnp.float32) * jnp.exp2(power - 15.0)


def dot(a, b):
    return jnp.dot(a, b, preferred_element_type=jnp.float32)


def copy_kernel(source, target):
    target[...] = source[...]


def at_hand_kernel(rows, cols, count, owners, tiles, notes, tiles_copy):
    notes[...] = jnp.zeros_like(notes)
    notes[0:1, 0 : rows.shape[1]] = rows[...]
    notes[1:2, 0 : cols.shape[1]] = cols[...]
    notes[2:3, 0:1] = count[...]
    notes[3:4, 0 : owners.shape[1]] = owners[...]
    tiles_copy[...] = tiles[...]


def each_tile(notes, tiles):
    total, size = tiles.shape[:2]
    for t in range(total):
        tile = jnp.where(t < notes[2, 0], tiles[t], jnp.zeros_like(tiles[t]))
        yield tile, *(
            pl.ds(pl.multiple_of(notes[which, t] * size, size), size) for which in (0, 1)
        )


def partial_kernel(rounds, sides, group, *refs):
    direct, relayed = refs[:rounds][::-1], refs[rounds : 2 * rounds][::-1]
    notes, tiles, partial, sent, q = refs[2 * rounds :]
    shard = direct[0].shape[0] // 2
    core, rows_of = own_place(sides, shard)
    for step in range(rounds):
        for ref, side in ((direct[step], core), (relayed[step], 1 - core)):
            q[rows_of(step, side, side), :] = ref[0:shard, :]
            q[rows_of(step, side, 1 - side), :] = ref[shard : 2 * shard, :]
    height = partial.shape[0]
    size = height // group
    partial[...] = jnp.zeros_like(partial)
    for tile, rows, cols in each_tile(notes, tiles):
        partial[rows, :] = partial[rows, :] + dot(tile, q[cols, :])
    powers = []
    for k in range(group):
        rows = slice(k * size, (k + 1) * size)
        sent[rows, :], power = coded(partial[rows, :])
        powers.append(power)
    powers.append(jnp.zeros((SCALE_ROWS - group, partial.shape[1]), jnp.float32))
    sent[height:, :] = jnp.concatenate(powers, axis=0).astype(jnp.int32).astype(jnp.int16)


def turned_kernel(notes, tiles, high, low, a):
    a[...] = jnp.zeros_like(a)
    for tile, rows, cols in each_tile(notes, tiles):
        a[rows, cols] = a[rows, cols] + tile.astype(jnp.float32)
    turned = a[...].T
    high[...] = turned.astype(high.dtype)
    low[...] = (turned - high[...].astype(jnp.float32)).astype(low.dtype)


def product_kernel(rounds, sides, group, *refs):
    partial, came, high, low, y = refs[:5]
    keep, give = refs[5 : 5 + rounds], refs[5 + rounds : 5 + 2 * rounds]
    z = refs[5 + 2 * rounds]
    height = partial.shape[0]
    size = height // group
    powers = came[height:, :].astype(jnp.int32).astype(jnp.float32)
    for k in range(group):
        rows = slice(k * size, (k + 1) * size)
        term = decoded(came[rows, :], powers[k : k + 1, :])
        y[rows, :] = (partial[rows, :] + term).astype(y.dtype)
    z[...] = dot(high[...], y[...]) + dot(low[...], y[...])
    shard = keep[0].shape[0] // 2
    core, rows_of = own_place(sides, shard)
    for step in range(rounds):
        for ref, side in ((keep[step], core), (give[step], 1 - core)):
            ref[0:shard, :] = z[rows_of(step, side, side), :]
            ref[shard : 2 * shard, :] = z[rows_of(step, side, 1 - side), :]


def owned_kernel(group, y, notes, y_out):
    size = y.shape[0] // group
    mine = group // 2
    for k in range(group):
        slot = notes[3, k]

        @pl.when(lax.div(slot, mine) == lax.axis_index("rows"))
        def _():
            at = pl.multiple_of(lax.rem(slot, mine) * size, size)
            y_out[pl.ds(at, size), :] = y[k * size : (k + 1) * size, :]


def paired(q_panel, tiles, tile_rows, tile_cols, tile_count, owner_map):
    devices = lax.axis_size("blk")
    chips = devices // 2
    rounds = chips // 2
    sides = sides_of(chips)
    shard, rank = q_panel.shape[1:]
    stack = tiles[0, 0]
    total, size = stack.shape[:2]
    group = owner_map.shape[1]
    width = devices * shard
    height = group * size
    across = [(0, 1), (1, 0)]
    sibling = [(i, i ^ 1) for i in range(devices)]
    vmem = pl.BlockSpec(memory_space=pltpu.VMEM)

    def to_chips(step):
        return [
            (2 * m + c, 2 * (m ^ sides[c][step]) + c)
            for m in range(chips)
            for c in range(2)
        ]

    def call(body, name, outs, args, scratch=()):
        return pl.pallas_call(
            body,
            out_shape=[jax.ShapeDtypeStruct(*out) for out in outs],
            in_specs=[vmem] * len(args),
            out_specs=[vmem] * len(outs),
            scratch_shapes=list(scratch),
            compiler_params=pltpu.CompilerParams(vmem_limit_bytes=VMEM_BYTES),
            name=name,
        )(*args)

    q_own = q_panel[0]
    q_sibling = lax.ppermute(q_own, "blk", sibling)
    (q_copy,) = call(copy_kernel, "own_rows", [(q_own.shape, q_own.dtype)], [q_own])
    block = jnp.concatenate([q_copy, q_sibling], axis=0)
    direct = [lax.ppermute(block, "blk", to_chips(step)) for step in range(rounds)]

    stack, direct[0] = lax.optimization_barrier((stack, direct[0]))
    notes, stack = call(
        at_hand_kernel,
        "at_hand",
        [((8, LANES), jnp.int32), (stack.shape, stack.dtype)],
        [
            tile_rows.reshape(1, total),
            tile_cols.reshape(1, total),
            tile_count,
            owner_map,
            stack,
        ],
    )
    direct[1], notes, stack = lax.optimization_barrier((direct[1], notes, stack))
    relayed = [lax.ppermute(one, "blk", sibling) for one in direct]

    partial, sent = call(
        lambda *refs: partial_kernel(rounds, sides, group, *refs),
        "partial",
        [((height, rank), jnp.float32), ((height + SCALE_ROWS, rank), jnp.int16)],
        [*direct[::-1], *relayed[::-1], notes, stack],
        [pltpu.VMEM((width, rank), q_own.dtype)],
    )
    came = lax.ppermute(sent, "rows", across)
    notes, stack, sent = lax.optimization_barrier((notes, stack, sent))
    turned = call(
        turned_kernel,
        "turned",
        [((width, height), stack.dtype)] * 2,
        [notes, stack],
        [pltpu.VMEM((height, width), jnp.float32)],
    )
    y, *pieces = call(
        lambda *refs: product_kernel(rounds, sides, group, *refs),
        "products",
        [((height, rank), jnp.bfloat16)]
        + [((2 * shard, rank), jnp.float32)] * (2 * rounds),
        [partial, came, *turned],
        [pltpu.VMEM((width, rank), jnp.float32)],
    )
    keep, give = pieces[:rounds], pieces[rounds:]
    given = [lax.ppermute(one, "blk", sibling) for one in give]
    arrived = [
        lax.ppermute(keep[step] + given[step], "blk", to_chips(step)) for step in range(rounds)
    ]
    y, arrived[0] = lax.optimization_barrier((y, arrived[0]))
    (y_owned,) = call(
        lambda *refs: owned_kernel(group, *refs),
        "owned",
        [((height // 2, rank), jnp.bfloat16)],
        [y, notes],
    )
    arrived[1], y_owned = lax.optimization_barrier((arrived[1], y_owned))
    summed = arrived[0]
    for step in range(1, rounds):
        summed = summed + arrived[step]
    z_share = summed[:shard] + lax.ppermute(summed[shard:], "blk", sibling)
    return (y_owned[None], z_share[None])


def general(q_panel, tiles, tile_rows, tile_cols, tile_count, owner_map):
    panel_rows = q_panel.shape[1]
    tile_stack = tiles[0, 0]
    tile_total = tile_stack.shape[0]
    tile_size = tile_stack.shape[1]
    group_blocks = owner_map.shape[1]
    class_blocks = panel_rows * lax.axis_size("blk") // tile_size
    column_ids = tile_cols[0, 0, :, 0]
    active = jnp.arange(tile_total, dtype=jnp.int32) < tile_count[0, 0]
    slot_of_tile = owner_map[0][tile_rows[0, 0]]
    slot_hit = slot_of_tile[:, None] == jnp.arange(group_blocks, dtype=jnp.int32)[None, :]
    column_hit = column_ids[:, None] == jnp.arange(class_blocks, dtype=jnp.int32)[None, :]
    placing = (slot_hit[:, :, None] & column_hit[:, None, :] & active[:, None, None]).astype(
        tile_stack.dtype
    )
    local_matrix = jnp.einsum(
        "tsc,tik->sick", placing, tile_stack, preferred_element_type=jnp.float32
    )
    local_matrix = local_matrix.reshape(group_blocks * tile_size, class_blocks * tile_size)
    rows_in = lax.all_gather(q_panel, "blk", axis=1, tiled=True)[0]
    flat_partial = jnp.dot(
        local_matrix, rows_in.astype(jnp.float32), precision=lax.Precision.HIGHEST
    )
    owned = lax.psum_scatter(flat_partial, "rows", scatter_dimension=0, tiled=True)
    y_owned = owned.astype(jnp.bfloat16)
    y_group = lax.all_gather(y_owned, "rows", axis=0, tiled=True)
    column_term = lax.dot_general(
        local_matrix,
        y_group.astype(jnp.float32),
        (((0,), (0,)), ((), ())),
        precision=lax.Precision.HIGHEST,
    )
    z_share = lax.psum_scatter(column_term, "blk", scatter_dimension=0, tiled=True)
    return (y_owned[None], z_share[None])


def solution(mesh):
    placed = (
        P("rows", "blk", None),
        P("blk", "rows", None, None, None),
        P("blk", "rows", None),
        P("blk", "rows", None, None),
        P("blk", "rows"),
        P("blk", None),
    )
    devices = mesh.shape["blk"]
    fits = mesh.shape["rows"] == 2 and devices >= 8 and devices & (devices - 1) == 0
    return jax.shard_map(
        paired if fits else general,
        mesh=mesh,
        in_specs=placed,
        out_specs=(P("blk", "rows", None), P("rows", "blk", None)),
        check_vma=False,
    )
```

```python
import jax
import jax.numpy as jnp
from jax import lax
from jax.experimental import pallas as pl
from jax.experimental.pallas import tpu as pltpu
from jax.sharding import PartitionSpec as P


LANES = 128
VMEM_BYTES = 24 << 20
PAIR_COST, TURNED_COST = 1 << 35, 1 << 31


def sides_of(chips):
    sides = ([], [])
    load = [0, 0]
    for k in sorted(range(2, chips), key=lambda k: -(k // 2 + k % 2)):
        open_sides = [c for c in range(2) if len(sides[c]) < chips // 2 - 1]
        c = min(open_sides, key=lambda c: load[c])
        sides[c].append(k)
        load[c] += k // 2 + k % 2
    return sides


def own_place(sides, shard):
    place = lax.axis_index("blk")
    core, chip = lax.rem(place, 2), lax.div(place, 2)

    def rows_at(offset, owner):
        which = lax.bitwise_xor(chip, offset)
        return pl.ds(pl.multiple_of(which * (2 * shard) + owner * shard, shard), shard)

    def rows_of(step, side, owner):
        return rows_at(jnp.where(side == 0, sides[0][step], sides[1][step]), owner)

    return core, rows_at, rows_of


def dot(a, b):
    return jnp.dot(a, b, preferred_element_type=jnp.float32)


def pair_kernel(q_own, q_far, pair):
    shard = q_own.shape[0]
    pair[0:shard, :] = q_own[...]
    pair[shard:, :] = q_far[...]


def front_kernel(rows, cols, count, owners, q_own, notes, q_copy):
    notes[...] = jnp.zeros_like(notes)
    notes[0:1, 0 : rows.shape[1]] = rows[...]
    notes[1:2, 0 : cols.shape[1]] = cols[...]
    notes[2:3, 0:1] = count[...]
    notes[3:4, 0 : owners.shape[1]] = owners[...]
    q_copy[...] = q_own[...]


def each_tile(notes, tiles):
    total, size = tiles.shape[:2]
    for t in range(total):
        tile = jnp.where(t < notes[2, 0], tiles[t], jnp.zeros_like(tiles[t]))
        yield tile, *(
            pl.ds(pl.multiple_of(notes[which, t] * size, size), size) for which in (0, 1)
        )


def add_tiles(total, notes, tiles, q):
    for tile, rows, cols in each_tile(notes, tiles):
        total[rows, :] = total[rows, :] + dot(tile, q[cols, :])


def near_kernel(rounds, sides, *refs):
    block, beside, *refs = refs
    direct, relayed = refs[:rounds][::-1], refs[rounds : 2 * rounds][::-1]
    notes, tiles, y, q_far, q_near = refs[2 * rounds :]
    shard = block.shape[0] // 4
    core, rows_at, rows_of = own_place(sides, shard)

    def put(ref, rows, other):
        for part, at in enumerate((rows, other)):
            low = 2 * part * shard
            q_near[at, :] = ref[low : low + shard, :]
            q_far[at, :] = ref[low + shard : low + 2 * shard, :]

    for ref, offset in ((block, 0), (beside, 1)):
        put(ref, rows_at(offset, core), rows_at(offset, 1 - core))
    for step in range(rounds):
        for ref, side in ((direct[step], core), (relayed[step], 1 - core)):
            put(ref, rows_of(step, side, side), rows_of(step, side, 1 - side))
    y[...] = jnp.zeros_like(y)
    add_tiles(y, notes, tiles, q_near)


def turned_kernel(notes, tiles, high, low, a):
    a[...] = jnp.zeros_like(a)
    for tile, rows, cols in each_tile(notes, tiles):
        a[rows, cols] = a[rows, cols] + tile.astype(jnp.float32)
    turned = a[...].T
    high[...] = turned.astype(high.dtype)
    low[...] = (turned - high[...].astype(jnp.float32)).astype(low.dtype)


def product_kernel(rounds, sides, *refs):
    y_near, q_far, far_notes, far_tiles, high, low, y = refs[:7]
    keep, give = refs[7 : 8 + rounds], refs[8 + rounds : 9 + 2 * rounds]
    total, z = refs[9 + 2 * rounds :]
    total[...] = y_near[...]
    add_tiles(total, far_notes, far_tiles, q_far)
    y[...] = total[...].astype(y.dtype)
    z[...] = dot(high[...], y[...]) + dot(low[...], y[...])
    shard = keep[0].shape[0] // 2
    core, rows_at, rows_of = own_place(sides, shard)
    for step in range(rounds):
        for ref, side in ((keep[step], core), (give[step], 1 - core)):
            ref[0:shard, :] = z[rows_of(step, side, side), :]
            ref[shard : 2 * shard, :] = z[rows_of(step, side, 1 - side), :]
    for ref, side in ((keep[rounds], core), (give[rounds], 1 - core)):
        ref[0:shard, :] = z[rows_at(0, side), :]
        ref[shard : 2 * shard, :] = z[rows_at(1, side), :]


def owned_kernel(group, y, notes, y_out):
    size = y.shape[0] // group
    mine = group // 2
    for k in range(group):
        slot = notes[3, k]

        @pl.when(lax.div(slot, mine) == lax.axis_index("rows"))
        def _():
            at = pl.multiple_of(lax.rem(slot, mine) * size, size)
            y_out[pl.ds(at, size), :] = y[k * size : (k + 1) * size, :]


def paired(q_panel, tiles, tile_rows, tile_cols, tile_count, owner_map):
    devices = lax.axis_size("blk")
    chips = devices // 2
    rounds = chips // 2 - 1
    sides = sides_of(chips)
    shard, rank = q_panel.shape[1:]
    stack = tiles[0, 0]
    total, size = stack.shape[:2]
    group = owner_map.shape[1]
    width = devices * shard
    height = group * size
    across = [(0, 1), (1, 0)]
    sibling = [(i, i ^ 1) for i in range(devices)]
    neighbour = [(i, i ^ 2) for i in range(devices)]
    vmem = pl.BlockSpec(memory_space=pltpu.VMEM)

    def to_chips(step):
        return [
            (2 * m + c, 2 * (m ^ sides[c][step]) + c)
            for m in range(chips)
            for c in range(2)
        ]

    def call(body, name, outs, args, scratch=(), cost=0):
        return pl.pallas_call(
            body,
            out_shape=[jax.ShapeDtypeStruct(*out) for out in outs],
            in_specs=[vmem] * len(args),
            out_specs=[vmem] * len(outs),
            scratch_shapes=list(scratch),
            compiler_params=pltpu.CompilerParams(vmem_limit_bytes=VMEM_BYTES),
            cost_estimate=pl.CostEstimate(flops=cost, bytes_accessed=0, transcendentals=0)
            if cost
            else None,
            name=name,
        )(*args)

    q_own = q_panel[0]
    q_far = lax.ppermute(q_own, "rows", across)
    far_tiles = lax.ppermute(stack, "rows", across)
    notes, q_copy = call(
        front_kernel,
        "front",
        [((8, LANES), jnp.int32), (q_own.shape, q_own.dtype)],
        [
            tile_rows.reshape(1, total),
            tile_cols.reshape(1, total),
            tile_count,
            owner_map,
            q_own,
        ],
    )
    (pair,) = call(
        pair_kernel,
        "pair",
        [((2 * shard, rank), q_own.dtype)],
        [q_copy, q_far],
        cost=PAIR_COST,
    )
    block = jnp.concatenate([pair, lax.ppermute(pair, "blk", sibling)], axis=0)
    direct = [lax.ppermute(block, "blk", to_chips(step)) for step in range(rounds)]
    beside = lax.ppermute(block, "blk", neighbour)

    stack, notes, direct[0] = lax.optimization_barrier((stack, notes, direct[0]))
    turned = call(
        turned_kernel,
        "turned",
        [((width, height), stack.dtype)] * 2,
        [notes, stack],
        [pltpu.VMEM((height, width), jnp.float32)],
        cost=TURNED_COST,
    )
    direct[1], *turned = lax.optimization_barrier((direct[1], *turned))
    far_notes = lax.ppermute(notes, "rows", across)
    relayed = [lax.ppermute(one, "blk", sibling) for one in direct]

    y_near, q_other = call(
        lambda *refs: near_kernel(rounds, sides, *refs),
        "near_products",
        [((height, rank), jnp.float32), ((width, rank), q_own.dtype)],
        [block, beside, *direct[::-1], *relayed[::-1], notes, stack],
        [pltpu.VMEM((width, rank), q_own.dtype)],
        cost=1,
    )
    y, *pieces = call(
        lambda *refs: product_kernel(rounds, sides, *refs),
        "products",
        [((height, rank), jnp.bfloat16)]
        + [((2 * shard, rank), jnp.float32)] * (2 * rounds + 2),
        [y_near, q_other, far_notes, far_tiles, *turned],
        [pltpu.VMEM((height, rank), jnp.float32), pltpu.VMEM((width, rank), jnp.float32)],
    )
    keep, give = pieces[: rounds + 1], pieces[rounds + 1 :]
    given = [lax.ppermute(one, "blk", sibling) for one in give]
    arrived = [
        lax.ppermute(keep[step] + given[step], "blk", to_chips(step)) for step in range(rounds)
    ]
    last = keep[rounds] + given[rounds]
    z_beside = lax.ppermute(last[shard:], "blk", neighbour)
    y, arrived[0] = lax.optimization_barrier((y, arrived[0]))
    (y_owned,) = call(
        lambda *refs: owned_kernel(group, *refs),
        "owned",
        [((height // 2, rank), jnp.bfloat16)],
        [y, notes],
    )
    arrived[1], y_owned = lax.optimization_barrier((arrived[1], y_owned))
    summed = arrived[0]
    for step in range(1, rounds):
        summed = summed + arrived[step]
    z_sibling = lax.ppermute(summed[shard:], "blk", sibling)
    z_share = (summed[:shard] + last[:shard]) + (z_sibling + z_beside)
    return (y_owned[None], z_share[None])


def general(q_panel, tiles, tile_rows, tile_cols, tile_count, owner_map):
    panel_rows = q_panel.shape[1]
    tile_stack = tiles[0, 0]
    tile_total = tile_stack.shape[0]
    tile_size = tile_stack.shape[1]
    group_blocks = owner_map.shape[1]
    class_blocks = panel_rows * lax.axis_size("blk") // tile_size
    column_ids = tile_cols[0, 0, :, 0]
    active = jnp.arange(tile_total, dtype=jnp.int32) < tile_count[0, 0]
    slot_of_tile = owner_map[0][tile_rows[0, 0]]
    slot_hit = slot_of_tile[:, None] == jnp.arange(group_blocks, dtype=jnp.int32)[None, :]
    column_hit = column_ids[:, None] == jnp.arange(class_blocks, dtype=jnp.int32)[None, :]
    placing = (slot_hit[:, :, None] & column_hit[:, None, :] & active[:, None, None]).astype(
        tile_stack.dtype
    )
    local_matrix = jnp.einsum(
        "tsc,tik->sick", placing, tile_stack, preferred_element_type=jnp.float32
    )
    local_matrix = local_matrix.reshape(group_blocks * tile_size, class_blocks * tile_size)
    rows_in = lax.all_gather(q_panel, "blk", axis=1, tiled=True)[0]
    flat_partial = jnp.dot(
        local_matrix, rows_in.astype(jnp.float32), precision=lax.Precision.HIGHEST
    )
    owned = lax.psum_scatter(flat_partial, "rows", scatter_dimension=0, tiled=True)
    y_owned = owned.astype(jnp.bfloat16)
    y_group = lax.all_gather(y_owned, "rows", axis=0, tiled=True)
    column_term = lax.dot_general(
        local_matrix,
        y_group.astype(jnp.float32),
        (((0,), (0,)), ((), ())),
        precision=lax.Precision.HIGHEST,
    )
    z_share = lax.psum_scatter(column_term, "blk", scatter_dimension=0, tiled=True)
    return (y_owned[None], z_share[None])


def solution(mesh):
    placed = (
        P("rows", "blk", None),
        P("blk", "rows", None, None, None),
        P("blk", "rows", None),
        P("blk", "rows", None, None),
        P("blk", "rows"),
        P("blk", None),
    )
    devices = mesh.shape["blk"]
    fits = mesh.shape["rows"] == 2 and devices >= 8 and devices & (devices - 1) == 0
    return jax.shard_map(
        paired if fits else general,
        mesh=mesh,
        in_specs=placed,
        out_specs=(P("blk", "rows", None), P("rows", "blk", None)),
        check_vma=False,
    )
```

```python
import jax
import jax.numpy as jnp
from jax import lax
from jax.experimental import pallas as pl
from jax.experimental.pallas import tpu as pltpu
from jax.sharding import PartitionSpec as P


LANES = 128
SCALE_ROWS = 16
VMEM_BYTES = 24 << 20
PAIR_COST, TURNED_COST = 1 << 35, 1 << 31


def sides_of(chips):
    return tuple(
        [k for k in reversed(range(2, chips)) if k.bit_count() % 2 == odd] for odd in (1, 0)
    )


def own_place(sides, shard):
    place = lax.axis_index("blk")
    core, chip = lax.rem(place, 2), lax.div(place, 2)

    def rows_at(offset, owner):
        which = lax.bitwise_xor(chip, offset)
        return pl.ds(pl.multiple_of(which * (2 * shard) + owner * shard, shard), shard)

    def rows_of(step, side, owner):
        return rows_at(jnp.where(side == 0, sides[0][step], sides[1][step]), owner)

    return core, rows_at, rows_of


def dot(a, b):
    return jnp.dot(a, b, preferred_element_type=jnp.float32)


def pair_kernel(q_own, q_far, pair):
    shard = q_own.shape[0]
    pair[0:shard, :] = q_own[...]
    pair[shard:, :] = q_far[...]


def front_kernel(rows, cols, count, owners, q_own, notes, q_copy):
    notes[...] = jnp.zeros_like(notes)
    notes[0:1, 0 : rows.shape[1]] = rows[...]
    notes[1:2, 0 : cols.shape[1]] = cols[...]
    notes[2:3, 0:1] = count[...]
    notes[3:4, 0 : owners.shape[1]] = owners[...]
    q_copy[...] = q_own[...]


def each_tile(notes, tiles):
    total, size = tiles.shape[:2]
    for t in range(total):
        tile = jnp.where(t < notes[2, 0], tiles[t], jnp.zeros_like(tiles[t]))
        yield tile, *(
            pl.ds(pl.multiple_of(notes[which, t] * size, size), size) for which in (0, 1)
        )


def coded_kernel(ours, given, sent):
    rows = ours.shape[0]
    x = ours[...] + given[...]
    top = jnp.max(jnp.abs(x), axis=0, keepdims=True)
    power = jnp.ceil(jnp.log2(jnp.maximum(top, 1e-30)))
    whole = jnp.clip(jnp.round(x * jnp.exp2(15.0 - power)), -32767.0, 32767.0)
    sent[0:rows, :] = whole.astype(jnp.int32).astype(jnp.int16)
    power = jnp.broadcast_to(power, (SCALE_ROWS, x.shape[1]))
    sent[rows:, :] = power.astype(jnp.int32).astype(jnp.int16)


def gather_kernel(*refs):
    *arrived, last, mine, theirs = refs
    shard = mine.shape[0]
    total = jnp.concatenate([last[0:shard, :], jnp.zeros_like(mine)], axis=0)
    for ref in arrived:
        x = ref[0 : 2 * shard, :].astype(jnp.int32).astype(jnp.float32)
        power = ref[2 * shard :, :].astype(jnp.int32).astype(jnp.float32)
        total = total + x * jnp.exp2(power[0:1, :] - 15.0)
    mine[...] = total[0:shard, :]
    theirs[...] = total[shard:, :]


def add_tiles(total, notes, tiles, q):
    for tile, rows, cols in each_tile(notes, tiles):
        total[rows, :] = total[rows, :] + dot(tile, q[cols, :])


def near_kernel(rounds, sides, *refs):
    block, beside, *refs = refs
    direct, relayed = refs[:rounds][::-1], refs[rounds : 2 * rounds][::-1]
    notes, tiles, y, q_far, q_near = refs[2 * rounds :]
    shard = block.shape[0] // 4
    core, rows_at, rows_of = own_place(sides, shard)

    def put(ref, rows, other):
        for part, at in enumerate((rows, other)):
            low = 2 * part * shard
            q_near[at, :] = ref[low : low + shard, :]
            q_far[at, :] = ref[low + shard : low + 2 * shard, :]

    for ref, offset in ((block, 0), (beside, 1)):
        put(ref, rows_at(offset, core), rows_at(offset, 1 - core))
    for step in range(rounds):
        for ref, side in ((direct[step], core), (relayed[step], 1 - core)):
            put(ref, rows_of(step, side, side), rows_of(step, side, 1 - side))
    y[...] = jnp.zeros_like(y)
    add_tiles(y, notes, tiles, q_near)


def turned_kernel(notes, tiles, high, low, a):
    a[...] = jnp.zeros_like(a)
    for tile, rows, cols in each_tile(notes, tiles):
        a[rows, cols] = a[rows, cols] + tile.astype(jnp.float32)
    turned = a[...].T
    high[...] = turned.astype(high.dtype)
    low[...] = (turned - high[...].astype(jnp.float32)).astype(low.dtype)


def product_kernel(rounds, sides, *refs):
    y_near, q_far, far_notes, far_tiles, high, low, y = refs[:7]
    keep, give = refs[7 : 8 + rounds], refs[8 + rounds : 9 + 2 * rounds]
    total, z = refs[9 + 2 * rounds :]
    total[...] = y_near[...]
    add_tiles(total, far_notes, far_tiles, q_far)
    y[...] = total[...].astype(y.dtype)
    z[...] = dot(high[...], y[...]) + dot(low[...], y[...])
    shard = keep[0].shape[0] // 2
    core, rows_at, rows_of = own_place(sides, shard)
    for step in range(rounds):
        for ref, side in ((keep[step], core), (give[step], 1 - core)):
            ref[0:shard, :] = z[rows_of(step, side, side), :]
            ref[shard : 2 * shard, :] = z[rows_of(step, side, 1 - side), :]
    for ref, side in ((keep[rounds], core), (give[rounds], 1 - core)):
        ref[0:shard, :] = z[rows_at(0, side), :]
        ref[shard : 2 * shard, :] = z[rows_at(1, side), :]


def owned_kernel(group, y, notes, y_out):
    size = y.shape[0] // group
    mine = group // 2
    for k in range(group):
        slot = notes[3, k]

        @pl.when(lax.div(slot, mine) == lax.axis_index("rows"))
        def _():
            at = pl.multiple_of(lax.rem(slot, mine) * size, size)
            y_out[pl.ds(at, size), :] = y[k * size : (k + 1) * size, :]


def paired(q_panel, tiles, tile_rows, tile_cols, tile_count, owner_map):
    devices = lax.axis_size("blk")
    chips = devices // 2
    rounds = chips // 2 - 1
    sides = sides_of(chips)
    shard, rank = q_panel.shape[1:]
    stack = tiles[0, 0]
    total, size = stack.shape[:2]
    group = owner_map.shape[1]
    width = devices * shard
    height = group * size
    across = [(0, 1), (1, 0)]
    sibling = [(i, i ^ 1) for i in range(devices)]
    neighbour = [(i, i ^ 2) for i in range(devices)]
    vmem = pl.BlockSpec(memory_space=pltpu.VMEM)

    def to_chips(step):
        return [
            (2 * m + c, 2 * (m ^ sides[c][step]) + c)
            for m in range(chips)
            for c in range(2)
        ]

    def call(body, name, outs, args, scratch=(), cost=0):
        return pl.pallas_call(
            body,
            out_shape=[jax.ShapeDtypeStruct(*out) for out in outs],
            in_specs=[vmem] * len(args),
            out_specs=[vmem] * len(outs),
            scratch_shapes=list(scratch),
            compiler_params=pltpu.CompilerParams(vmem_limit_bytes=VMEM_BYTES),
            cost_estimate=pl.CostEstimate(flops=cost, bytes_accessed=0, transcendentals=0)
            if cost
            else None,
            name=name,
        )(*args)

    q_own = q_panel[0]
    q_far = lax.ppermute(q_own, "rows", across)
    far_tiles = lax.ppermute(stack, "rows", across)
    notes, q_copy = call(
        front_kernel,
        "front",
        [((8, LANES), jnp.int32), (q_own.shape, q_own.dtype)],
        [
            tile_rows.reshape(1, total),
            tile_cols.reshape(1, total),
            tile_count,
            owner_map,
            q_own,
        ],
    )
    (pair,) = call(
        pair_kernel,
        "pair",
        [((2 * shard, rank), q_own.dtype)],
        [q_copy, q_far],
        cost=PAIR_COST,
    )
    block = jnp.concatenate([pair, lax.ppermute(pair, "blk", sibling)], axis=0)
    direct = [lax.ppermute(block, "blk", to_chips(step)) for step in range(rounds)]
    beside = lax.ppermute(block, "blk", neighbour)

    stack, notes, direct[0] = lax.optimization_barrier((stack, notes, direct[0]))
    turned = call(
        turned_kernel,
        "turned",
        [((width, height), stack.dtype)] * 2,
        [notes, stack],
        [pltpu.VMEM((height, width), jnp.float32)],
        cost=TURNED_COST,
    )
    direct[1], *turned = lax.optimization_barrier((direct[1], *turned))
    far_notes = lax.ppermute(notes, "rows", across)
    relayed = [lax.ppermute(one, "blk", sibling) for one in direct]

    y_near, q_other = call(
        lambda *refs: near_kernel(rounds, sides, *refs),
        "near_products",
        [((height, rank), jnp.float32), ((width, rank), q_own.dtype)],
        [block, beside, *direct[::-1], *relayed[::-1], notes, stack],
        [pltpu.VMEM((width, rank), q_own.dtype)],
        cost=1,
    )
    y, *pieces = call(
        lambda *refs: product_kernel(rounds, sides, *refs),
        "products",
        [((height, rank), jnp.bfloat16)]
        + [((2 * shard, rank), jnp.float32)] * (2 * rounds + 2),
        [y_near, q_other, far_notes, far_tiles, *turned],
        [pltpu.VMEM((height, rank), jnp.float32), pltpu.VMEM((width, rank), jnp.float32)],
    )
    keep, give = pieces[: rounds + 1], pieces[rounds + 1 :]
    given = [lax.ppermute(one, "blk", sibling) for one in give]
    arrived = []
    for step in range(rounds):
        (sent,) = call(
            coded_kernel,
            "coded",
            [((2 * shard + SCALE_ROWS, rank), jnp.int16)],
            [keep[step], given[step]],
        )
        arrived.append(lax.ppermute(sent, "blk", to_chips(step)))
    last = keep[rounds] + given[rounds]
    z_beside = lax.ppermute(last[shard:], "blk", neighbour)
    y, arrived[0] = lax.optimization_barrier((y, arrived[0]))
    (y_owned,) = call(
        lambda *refs: owned_kernel(group, *refs),
        "owned",
        [((height // 2, rank), jnp.bfloat16)],
        [y, notes],
    )
    arrived[1], y_owned = lax.optimization_barrier((arrived[1], y_owned))
    z_mine, z_theirs = call(
        gather_kernel,
        "gathered",
        [((shard, rank), jnp.float32)] * 2,
        [*arrived, last],
    )
    z_share = z_mine + (lax.ppermute(z_theirs, "blk", sibling) + z_beside)
    return (y_owned[None], z_share[None])


def general(q_panel, tiles, tile_rows, tile_cols, tile_count, owner_map):
    panel_rows = q_panel.shape[1]
    tile_stack = tiles[0, 0]
    tile_total = tile_stack.shape[0]
    tile_size = tile_stack.shape[1]
    group_blocks = owner_map.shape[1]
    class_blocks = panel_rows * lax.axis_size("blk") // tile_size
    column_ids = tile_cols[0, 0, :, 0]
    active = jnp.arange(tile_total, dtype=jnp.int32) < tile_count[0, 0]
    slot_of_tile = owner_map[0][tile_rows[0, 0]]
    slot_hit = slot_of_tile[:, None] == jnp.arange(group_blocks, dtype=jnp.int32)[None, :]
    column_hit = column_ids[:, None] == jnp.arange(class_blocks, dtype=jnp.int32)[None, :]
    placing = (slot_hit[:, :, None] & column_hit[:, None, :] & active[:, None, None]).astype(
        tile_stack.dtype
    )
    local_matrix = jnp.einsum(
        "tsc,tik->sick", placing, tile_stack, preferred_element_type=jnp.float32
    )
    local_matrix = local_matrix.reshape(group_blocks * tile_size, class_blocks * tile_size)
    rows_in = lax.all_gather(q_panel, "blk", axis=1, tiled=True)[0]
    flat_partial = jnp.dot(
        local_matrix, rows_in.astype(jnp.float32), precision=lax.Precision.HIGHEST
    )
    owned = lax.psum_scatter(flat_partial, "rows", scatter_dimension=0, tiled=True)
    y_owned = owned.astype(jnp.bfloat16)
    y_group = lax.all_gather(y_owned, "rows", axis=0, tiled=True)
    column_term = lax.dot_general(
        local_matrix,
        y_group.astype(jnp.float32),
        (((0,), (0,)), ((), ())),
        precision=lax.Precision.HIGHEST,
    )
    z_share = lax.psum_scatter(column_term, "blk", scatter_dimension=0, tiled=True)
    return (y_owned[None], z_share[None])


def solution(mesh):
    placed = (
        P("rows", "blk", None),
        P("blk", "rows", None, None, None),
        P("blk", "rows", None),
        P("blk", "rows", None, None),
        P("blk", "rows"),
        P("blk", None),
    )
    devices = mesh.shape["blk"]
    fits = mesh.shape["rows"] == 2 and devices >= 8 and devices & (devices - 1) == 0
    return jax.shard_map(
        paired if fits else general,
        mesh=mesh,
        in_specs=placed,
        out_specs=(P("blk", "rows", None), P("rows", "blk", None)),
        check_vma=False,
    )
```

```python
import jax
import jax.numpy as jnp
from jax import lax
from jax.experimental import pallas as pl
from jax.experimental.pallas import tpu as pltpu
from jax.sharding import PartitionSpec as P


LANES = 128
SCALE_ROWS = 16
VMEM_BYTES = 24 << 20
PAIR_COST, TURNED_COST = 1 << 35, 1 << 31


def sides_of(chips):
    return tuple(
        [k for k in reversed(range(2, chips)) if k.bit_count() % 2 == odd] for odd in (1, 0)
    )


def own_place(sides, shard):
    place = lax.axis_index("blk")
    core, chip = lax.rem(place, 2), lax.div(place, 2)

    def rows_at(offset, owner):
        which = lax.bitwise_xor(chip, offset)
        return pl.ds(pl.multiple_of(which * (2 * shard) + owner * shard, shard), shard)

    def rows_of(step, side, owner):
        return rows_at(jnp.where(side == 0, sides[0][step], sides[1][step]), owner)

    return core, rows_at, rows_of


def dot(a, b):
    return jnp.dot(a, b, preferred_element_type=jnp.float32)


def pair_kernel(q_own, q_far, pair):
    shard = q_own.shape[0]
    pair[0:shard, :] = q_own[...]
    pair[shard:, :] = q_far[...]


def front_kernel(rows, cols, count, owners, q_own, notes, q_copy):
    notes[...] = jnp.zeros_like(notes)
    notes[0:1, 0 : rows.shape[1]] = rows[...]
    notes[1:2, 0 : cols.shape[1]] = cols[...]
    notes[2:3, 0:1] = count[...]
    notes[3:4, 0 : owners.shape[1]] = owners[...]
    q_copy[...] = q_own[...]


def each_tile(notes, tiles):
    total, size = tiles.shape[:2]
    for t in range(total):
        tile = jnp.where(t < notes[2, 0], tiles[t], jnp.zeros_like(tiles[t]))
        yield tile, *(
            pl.ds(pl.multiple_of(notes[which, t] * size, size), size) for which in (0, 1)
        )


def coded_kernel(ours, given, sent):
    rows = ours.shape[0]
    x = ours[...] + given[...]
    top = jnp.max(jnp.abs(x), axis=0, keepdims=True)
    power = jnp.ceil(jnp.log2(jnp.maximum(top, 1e-30)))
    whole = jnp.clip(jnp.round(x * jnp.exp2(15.0 - power)), -32767.0, 32767.0)
    sent[0:rows, :] = whole.astype(jnp.int32).astype(jnp.int16)
    power = jnp.broadcast_to(power, (SCALE_ROWS, x.shape[1]))
    sent[rows:, :] = power.astype(jnp.int32).astype(jnp.int16)


def gather_kernel(*refs):
    *arrived, last, mine, theirs = refs
    shard = mine.shape[0]
    total = jnp.concatenate([last[0:shard, :], jnp.zeros_like(mine)], axis=0)
    for ref in arrived:
        x = ref[0 : 2 * shard, :].astype(jnp.int32).astype(jnp.float32)
        power = ref[2 * shard :, :].astype(jnp.int32).astype(jnp.float32)
        total = total + x * jnp.exp2(power[0:1, :] - 15.0)
    mine[...] = total[0:shard, :]
    theirs[...] = total[shard:, :]


def add_tiles(total, notes, tiles, q):
    for tile, rows, cols in each_tile(notes, tiles):
        total[rows, :] = total[rows, :] + dot(tile, q[cols, :])


def near_kernel(rounds, sides, *refs):
    block, beside, *refs = refs
    direct, relayed = refs[:rounds][::-1], refs[rounds : 2 * rounds][::-1]
    notes, tiles, y, q_far, q_near = refs[2 * rounds :]
    shard = block.shape[0] // 4
    core, rows_at, rows_of = own_place(sides, shard)

    def put(ref, rows, other):
        for part, at in enumerate((rows, other)):
            low = 2 * part * shard
            q_near[at, :] = ref[low : low + shard, :]
            q_far[at, :] = ref[low + shard : low + 2 * shard, :]

    for ref, offset in ((block, 0), (beside, 1)):
        put(ref, rows_at(offset, core), rows_at(offset, 1 - core))
    for step in range(rounds):
        for ref, side in ((direct[step], core), (relayed[step], 1 - core)):
            put(ref, rows_of(step, side, side), rows_of(step, side, 1 - side))
    y[...] = jnp.zeros_like(y)
    add_tiles(y, notes, tiles, q_near)


def turned_kernel(notes, tiles, high, low, a):
    a[...] = jnp.zeros_like(a)
    for tile, rows, cols in each_tile(notes, tiles):
        a[rows, cols] = a[rows, cols] + tile.astype(jnp.float32)
    turned = a[...].T
    high[...] = turned.astype(high.dtype)
    low[...] = (turned - high[...].astype(jnp.float32)).astype(low.dtype)


def product_kernel(rounds, sides, *refs):
    y_near, q_far, far_notes, far_tiles, high, low, y = refs[:7]
    keep, give = refs[7 : 8 + rounds], refs[8 + rounds : 9 + 2 * rounds]
    total, z = refs[9 + 2 * rounds :]
    total[...] = y_near[...]
    add_tiles(total, far_notes, far_tiles, q_far)
    y[...] = total[...].astype(y.dtype)
    z[...] = dot(high[...], y[...]) + dot(low[...], y[...])
    shard = keep[0].shape[0] // 2
    core, rows_at, rows_of = own_place(sides, shard)
    for step in range(rounds):
        for ref, side in ((keep[step], core), (give[step], 1 - core)):
            ref[0:shard, :] = z[rows_of(step, side, side), :]
            ref[shard : 2 * shard, :] = z[rows_of(step, side, 1 - side), :]
    for ref, side in ((keep[rounds], core), (give[rounds], 1 - core)):
        ref[0:shard, :] = z[rows_at(0, side), :]
        ref[shard : 2 * shard, :] = z[rows_at(1, side), :]


def owned_kernel(group, y, notes, y_out):
    size = y.shape[0] // group
    mine = group // 2
    for k in range(group):
        slot = notes[3, k]

        @pl.when(lax.div(slot, mine) == lax.axis_index("rows"))
        def _():
            at = pl.multiple_of(lax.rem(slot, mine) * size, size)
            y_out[pl.ds(at, size), :] = y[k * size : (k + 1) * size, :]


def paired(q_panel, tiles, tile_rows, tile_cols, tile_count, owner_map):
    devices = lax.axis_size("blk")
    chips = devices // 2
    rounds = chips // 2 - 1
    sides = sides_of(chips)
    shard, rank = q_panel.shape[1:]
    stack = tiles[0, 0]
    total, size = stack.shape[:2]
    group = owner_map.shape[1]
    width = devices * shard
    height = group * size
    across = [(0, 1), (1, 0)]
    sibling = [(i, i ^ 1) for i in range(devices)]
    neighbour = [(i, i ^ 2) for i in range(devices)]
    vmem = pl.BlockSpec(memory_space=pltpu.VMEM)

    def to_chips(step):
        return [
            (2 * m + c, 2 * (m ^ sides[c][step]) + c)
            for m in range(chips)
            for c in range(2)
        ]

    def call(body, name, outs, args, scratch=(), cost=0):
        return pl.pallas_call(
            body,
            out_shape=[jax.ShapeDtypeStruct(*out) for out in outs],
            in_specs=[vmem] * len(args),
            out_specs=[vmem] * len(outs),
            scratch_shapes=list(scratch),
            compiler_params=pltpu.CompilerParams(vmem_limit_bytes=VMEM_BYTES),
            cost_estimate=pl.CostEstimate(flops=cost, bytes_accessed=0, transcendentals=0)
            if cost
            else None,
            name=name,
        )(*args)

    q_own = q_panel[0]
    q_far = lax.ppermute(q_own, "rows", across)
    far_tiles = lax.ppermute(stack, "rows", across)
    notes, q_copy = call(
        front_kernel,
        "front",
        [((8, LANES), jnp.int32), (q_own.shape, q_own.dtype)],
        [
            tile_rows.reshape(1, total),
            tile_cols.reshape(1, total),
            tile_count,
            owner_map,
            q_own,
        ],
    )
    (pair,) = call(
        pair_kernel,
        "pair",
        [((2 * shard, rank), q_own.dtype)],
        [q_copy, q_far],
        cost=PAIR_COST,
    )
    block = jnp.concatenate([pair, lax.ppermute(pair, "blk", sibling)], axis=0)
    direct = [lax.ppermute(block, "blk", to_chips(step)) for step in range(rounds)]
    beside = lax.ppermute(block, "blk", neighbour)

    stack, notes, direct[0] = lax.optimization_barrier((stack, notes, direct[0]))
    turned = call(
        turned_kernel,
        "turned",
        [((width, height), stack.dtype)] * 2,
        [notes, stack],
        [pltpu.VMEM((height, width), jnp.float32)],
        cost=TURNED_COST,
    )
    far_notes = lax.ppermute(notes, "rows", across)
    relayed = [lax.ppermute(one, "blk", sibling) for one in direct]

    y_near, q_other = call(
        lambda *refs: near_kernel(rounds, sides, *refs),
        "near_products",
        [((height, rank), jnp.float32), ((width, rank), q_own.dtype)],
        [block, beside, *direct[::-1], *relayed[::-1], notes, stack],
        [pltpu.VMEM((width, rank), q_own.dtype)],
        cost=1,
    )
    y, *pieces = call(
        lambda *refs: product_kernel(rounds, sides, *refs),
        "products",
        [((height, rank), jnp.bfloat16)]
        + [((2 * shard, rank), jnp.float32)] * (2 * rounds + 2),
        [y_near, q_other, far_notes, far_tiles, *turned],
        [pltpu.VMEM((height, rank), jnp.float32), pltpu.VMEM((width, rank), jnp.float32)],
    )
    keep, give = pieces[: rounds + 1], pieces[rounds + 1 :]
    given = [lax.ppermute(one, "blk", sibling) for one in give]
    arrived = []
    for step in range(rounds):
        (sent,) = call(
            coded_kernel,
            "coded",
            [((2 * shard + SCALE_ROWS, rank), jnp.int16)],
            [keep[step], given[step]],
        )
        arrived.append(lax.ppermute(sent, "blk", to_chips(step)))
    last = keep[rounds] + given[rounds]
    z_beside = lax.ppermute(last[shard:], "blk", neighbour)
    y, arrived[0] = lax.optimization_barrier((y, arrived[0]))
    (y_owned,) = call(
        lambda *refs: owned_kernel(group, *refs),
        "owned",
        [((height // 2, rank), jnp.bfloat16)],
        [y, notes],
    )
    arrived[1], y_owned = lax.optimization_barrier((arrived[1], y_owned))
    z_mine, z_theirs = call(
        gather_kernel,
        "gathered",
        [((shard, rank), jnp.float32)] * 2,
        [*arrived, last],
    )
    z_share = z_mine + (lax.ppermute(z_theirs, "blk", sibling) + z_beside)
    return (y_owned[None], z_share[None])


def general(q_panel, tiles, tile_rows, tile_cols, tile_count, owner_map):
    panel_rows = q_panel.shape[1]
    tile_stack = tiles[0, 0]
    tile_total = tile_stack.shape[0]
    tile_size = tile_stack.shape[1]
    group_blocks = owner_map.shape[1]
    class_blocks = panel_rows * lax.axis_size("blk") // tile_size
    column_ids = tile_cols[0, 0, :, 0]
    active = jnp.arange(tile_total, dtype=jnp.int32) < tile_count[0, 0]
    slot_of_tile = owner_map[0][tile_rows[0, 0]]
    slot_hit = slot_of_tile[:, None] == jnp.arange(group_blocks, dtype=jnp.int32)[None, :]
    column_hit = column_ids[:, None] == jnp.arange(class_blocks, dtype=jnp.int32)[None, :]
    placing = (slot_hit[:, :, None] & column_hit[:, None, :] & active[:, None, None]).astype(
        tile_stack.dtype
    )
    local_matrix = jnp.einsum(
        "tsc,tik->sick", placing, tile_stack, preferred_element_type=jnp.float32
    )
    local_matrix = local_matrix.reshape(group_blocks * tile_size, class_blocks * tile_size)
    rows_in = lax.all_gather(q_panel, "blk", axis=1, tiled=True)[0]
    flat_partial = jnp.dot(
        local_matrix, rows_in.astype(jnp.float32), precision=lax.Precision.HIGHEST
    )
    owned = lax.psum_scatter(flat_partial, "rows", scatter_dimension=0, tiled=True)
    y_owned = owned.astype(jnp.bfloat16)
    y_group = lax.all_gather(y_owned, "rows", axis=0, tiled=True)
    column_term = lax.dot_general(
        local_matrix,
        y_group.astype(jnp.float32),
        (((0,), (0,)), ((), ())),
        precision=lax.Precision.HIGHEST,
    )
    z_share = lax.psum_scatter(column_term, "blk", scatter_dimension=0, tiled=True)
    return (y_owned[None], z_share[None])


def solution(mesh):
    placed = (
        P("rows", "blk", None),
        P("blk", "rows", None, None, None),
        P("blk", "rows", None),
        P("blk", "rows", None, None),
        P("blk", "rows"),
        P("blk", None),
    )
    devices = mesh.shape["blk"]
    fits = mesh.shape["rows"] == 2 and devices >= 8 and devices & (devices - 1) == 0
    return jax.shard_map(
        paired if fits else general,
        mesh=mesh,
        in_specs=placed,
        out_specs=(P("blk", "rows", None), P("rows", "blk", None)),
        check_vma=False,
    )
```

```python
import jax
import jax.numpy as jnp
from jax import lax
from jax.experimental import pallas as pl
from jax.experimental.pallas import tpu as pltpu
from jax.sharding import PartitionSpec as P


LANES = 128
SCALE_ROWS = 16
VMEM_BYTES = 24 << 20
PAIR_COST, TURNED_COST = 1 << 35, 1 << 31


def sides_of(chips):
    return tuple(
        [k for k in reversed(range(2, chips)) if k.bit_count() % 2 == odd] for odd in (1, 0)
    )


def own_place(sides, shard):
    place = lax.axis_index("blk")
    core, chip = lax.rem(place, 2), lax.div(place, 2)

    def rows_at(offset, owner):
        which = lax.bitwise_xor(chip, offset)
        return pl.ds(pl.multiple_of(which * (2 * shard) + owner * shard, shard), shard)

    def rows_of(step, side, owner):
        return rows_at(jnp.where(side == 0, sides[0][step], sides[1][step]), owner)

    return core, rows_at, rows_of


def dot(a, b):
    return jnp.dot(a, b, preferred_element_type=jnp.float32)


def pair_kernel(q_own, q_far, pair):
    shard = q_own.shape[0]
    pair[0:shard, :] = q_own[...]
    pair[shard:, :] = q_far[...]


def front_kernel(rows, cols, count, owners, q_own, notes, q_copy):
    notes[...] = jnp.zeros_like(notes)
    notes[0:1, 0 : rows.shape[1]] = rows[...]
    notes[1:2, 0 : cols.shape[1]] = cols[...]
    notes[2:3, 0:1] = count[...]
    notes[3:4, 0 : owners.shape[1]] = owners[...]
    q_copy[...] = q_own[...]


def each_tile(notes, tiles):
    total, size = tiles.shape[:2]
    for t in range(total):
        tile = jnp.where(t < notes[2, 0], tiles[t], jnp.zeros_like(tiles[t]))
        yield tile, *(
            pl.ds(pl.multiple_of(notes[which, t] * size, size), size) for which in (0, 1)
        )


def coded_kernel(step, sides, z, given, sent):
    rows = given.shape[0]
    core, _, rows_of = own_place(sides, rows // 2)
    ours = [z[rows_of(step, core, owner), :] for owner in (core, 1 - core)]
    x = jnp.concatenate(ours, axis=0) + given[...]
    top = jnp.max(jnp.abs(x), axis=0, keepdims=True)
    power = jnp.ceil(jnp.log2(jnp.maximum(top, 1e-30)))
    whole = jnp.clip(jnp.round(x * jnp.exp2(15.0 - power)), -32767.0, 32767.0)
    sent[0:rows, :] = whole.astype(jnp.int32).astype(jnp.int16)
    power = jnp.broadcast_to(power, (SCALE_ROWS, x.shape[1]))
    sent[rows:, :] = power.astype(jnp.int32).astype(jnp.int16)


def last_kernel(sides, z, given, last):
    shard = last.shape[0] // 2
    core, rows_at, _ = own_place(sides, shard)
    last[0:shard, :] = z[rows_at(0, core), :] + given[0:shard, :]
    last[shard:, :] = z[rows_at(1, core), :] + given[shard:, :]


def gather_kernel(*refs):
    *arrived, last, mine, theirs = refs
    shard = mine.shape[0]
    total = jnp.concatenate([last[0:shard, :], jnp.zeros_like(mine)], axis=0)
    for ref in arrived:
        x = ref[0 : 2 * shard, :].astype(jnp.int32).astype(jnp.float32)
        power = ref[2 * shard :, :].astype(jnp.int32).astype(jnp.float32)
        total = total + x * jnp.exp2(power[0:1, :] - 15.0)
    mine[...] = total[0:shard, :]
    theirs[...] = total[shard:, :]


def add_tiles(total, notes, tiles, q):
    for tile, rows, cols in each_tile(notes, tiles):
        total[rows, :] = total[rows, :] + dot(tile, q[cols, :])


def near_kernel(rounds, sides, *refs):
    block, beside, *refs = refs
    direct, relayed = refs[:rounds][::-1], refs[rounds : 2 * rounds][::-1]
    notes, tiles, y, q_far, q_near = refs[2 * rounds :]
    shard = block.shape[0] // 4
    core, rows_at, rows_of = own_place(sides, shard)

    def put(ref, rows, other):
        for part, at in enumerate((rows, other)):
            low = 2 * part * shard
            q_near[at, :] = ref[low : low + shard, :]
            q_far[at, :] = ref[low + shard : low + 2 * shard, :]

    for ref, offset in ((block, 0), (beside, 1)):
        put(ref, rows_at(offset, core), rows_at(offset, 1 - core))
    for step in range(rounds):
        for ref, side in ((direct[step], core), (relayed[step], 1 - core)):
            put(ref, rows_of(step, side, side), rows_of(step, side, 1 - side))
    y[...] = jnp.zeros_like(y)
    add_tiles(y, notes, tiles, q_near)


def turned_kernel(notes, tiles, high, low, a):
    a[...] = jnp.zeros_like(a)
    for tile, rows, cols in each_tile(notes, tiles):
        a[rows, cols] = a[rows, cols] + tile.astype(jnp.float32)
    turned = a[...].T
    high[...] = turned.astype(high.dtype)
    low[...] = (turned - high[...].astype(jnp.float32)).astype(low.dtype)


def product_kernel(rounds, sides, *refs):
    y_near, q_far, far_notes, far_tiles, high, low, y = refs[:7]
    z, *give, total = refs[7:]
    total[...] = y_near[...]
    add_tiles(total, far_notes, far_tiles, q_far)
    y[...] = total[...].astype(y.dtype)
    z[...] = dot(high[...], y[...]) + dot(low[...], y[...])
    shard = give[0].shape[0] // 2
    core, rows_at, rows_of = own_place(sides, shard)
    side = 1 - core
    for step in range(rounds):
        give[step][0:shard, :] = z[rows_of(step, side, side), :]
        give[step][shard : 2 * shard, :] = z[rows_of(step, side, core), :]
    give[rounds][0:shard, :] = z[rows_at(0, side), :]
    give[rounds][shard : 2 * shard, :] = z[rows_at(1, side), :]


def owned_kernel(group, y, notes, y_out):
    size = y.shape[0] // group
    mine = group // 2
    for k in range(group):
        slot = notes[3, k]

        @pl.when(lax.div(slot, mine) == lax.axis_index("rows"))
        def _():
            at = pl.multiple_of(lax.rem(slot, mine) * size, size)
            y_out[pl.ds(at, size), :] = y[k * size : (k + 1) * size, :]


def paired(q_panel, tiles, tile_rows, tile_cols, tile_count, owner_map):
    devices = lax.axis_size("blk")
    chips = devices // 2
    rounds = chips // 2 - 1
    sides = sides_of(chips)
    shard, rank = q_panel.shape[1:]
    stack = tiles[0, 0]
    total, size = stack.shape[:2]
    group = owner_map.shape[1]
    width = devices * shard
    height = group * size
    across = [(0, 1), (1, 0)]
    sibling = [(i, i ^ 1) for i in range(devices)]
    neighbour = [(i, i ^ 2) for i in range(devices)]
    vmem = pl.BlockSpec(memory_space=pltpu.VMEM)

    def to_chips(step):
        return [
            (2 * m + c, 2 * (m ^ sides[c][step]) + c)
            for m in range(chips)
            for c in range(2)
        ]

    def call(body, name, outs, args, scratch=(), cost=0):
        return pl.pallas_call(
            body,
            out_shape=[jax.ShapeDtypeStruct(*out) for out in outs],
            in_specs=[vmem] * len(args),
            out_specs=[vmem] * len(outs),
            scratch_shapes=list(scratch),
            compiler_params=pltpu.CompilerParams(vmem_limit_bytes=VMEM_BYTES),
            cost_estimate=pl.CostEstimate(flops=cost, bytes_accessed=0, transcendentals=0)
            if cost
            else None,
            name=name,
        )(*args)

    q_own = q_panel[0]
    q_far = lax.ppermute(q_own, "rows", across)
    far_tiles = lax.ppermute(stack, "rows", across)
    notes, q_copy = call(
        front_kernel,
        "front",
        [((8, LANES), jnp.int32), (q_own.shape, q_own.dtype)],
        [
            tile_rows.reshape(1, total),
            tile_cols.reshape(1, total),
            tile_count,
            owner_map,
            q_own,
        ],
    )
    (pair,) = call(
        pair_kernel,
        "pair",
        [((2 * shard, rank), q_own.dtype)],
        [q_copy, q_far],
        cost=PAIR_COST,
    )
    block = jnp.concatenate([pair, lax.ppermute(pair, "blk", sibling)], axis=0)
    direct = [lax.ppermute(block, "blk", to_chips(step)) for step in range(rounds)]
    beside = lax.ppermute(block, "blk", neighbour)

    stack, direct[0] = lax.optimization_barrier((stack, direct[0]))
    turned = call(
        turned_kernel,
        "turned",
        [((width, height), stack.dtype)] * 2,
        [notes, stack],
        [pltpu.VMEM((height, width), jnp.float32)],
        cost=TURNED_COST,
    )
    far_notes = lax.ppermute(notes, "rows", across)
    relayed = [lax.ppermute(one, "blk", sibling) for one in direct]

    y_near, q_other = call(
        lambda *refs: near_kernel(rounds, sides, *refs),
        "near_products",
        [((height, rank), jnp.float32), ((width, rank), q_own.dtype)],
        [block, beside, *direct[::-1], *relayed[::-1], notes, stack],
        [pltpu.VMEM((width, rank), q_own.dtype)],
        cost=1,
    )
    y, z, *give = call(
        lambda *refs: product_kernel(rounds, sides, *refs),
        "products",
        [((height, rank), jnp.bfloat16), ((width, rank), jnp.float32)]
        + [((2 * shard, rank), jnp.float32)] * (rounds + 1),
        [y_near, q_other, far_notes, far_tiles, *turned],
        [pltpu.VMEM((height, rank), jnp.float32)],
    )
    given = [lax.ppermute(one, "blk", sibling) for one in give]
    arrived = []
    for step in range(rounds):
        (sent,) = call(
            lambda *refs, step=step: coded_kernel(step, sides, *refs),
            "coded",
            [((2 * shard + SCALE_ROWS, rank), jnp.int16)],
            [z, given[step]],
        )
        arrived.append(lax.ppermute(sent, "blk", to_chips(step)))
    (last,) = call(
        lambda *refs: last_kernel(sides, *refs),
        "last",
        [((2 * shard, rank), jnp.float32)],
        [z, given[rounds]],
    )
    z_beside = lax.ppermute(last[shard:], "blk", neighbour)
    y, arrived[0] = lax.optimization_barrier((y, arrived[0]))
    (y_owned,) = call(
        lambda *refs: owned_kernel(group, *refs),
        "owned",
        [((height // 2, rank), jnp.bfloat16)],
        [y, notes],
    )
    arrived[1], y_owned = lax.optimization_barrier((arrived[1], y_owned))
    z_mine, z_theirs = call(
        gather_kernel,
        "gathered",
        [((shard, rank), jnp.float32)] * 2,
        [*arrived, last],
    )
    z_share = z_mine + (lax.ppermute(z_theirs, "blk", sibling) + z_beside)
    return (y_owned[None], z_share[None])


def general(q_panel, tiles, tile_rows, tile_cols, tile_count, owner_map):
    panel_rows = q_panel.shape[1]
    tile_stack = tiles[0, 0]
    tile_total = tile_stack.shape[0]
    tile_size = tile_stack.shape[1]
    group_blocks = owner_map.shape[1]
    class_blocks = panel_rows * lax.axis_size("blk") // tile_size
    column_ids = tile_cols[0, 0, :, 0]
    active = jnp.arange(tile_total, dtype=jnp.int32) < tile_count[0, 0]
    slot_of_tile = owner_map[0][tile_rows[0, 0]]
    slot_hit = slot_of_tile[:, None] == jnp.arange(group_blocks, dtype=jnp.int32)[None, :]
    column_hit = column_ids[:, None] == jnp.arange(class_blocks, dtype=jnp.int32)[None, :]
    placing = (slot_hit[:, :, None] & column_hit[:, None, :] & active[:, None, None]).astype(
        tile_stack.dtype
    )
    local_matrix = jnp.einsum(
        "tsc,tik->sick", placing, tile_stack, preferred_element_type=jnp.float32
    )
    local_matrix = local_matrix.reshape(group_blocks * tile_size, class_blocks * tile_size)
    rows_in = lax.all_gather(q_panel, "blk", axis=1, tiled=True)[0]
    flat_partial = jnp.dot(
        local_matrix, rows_in.astype(jnp.float32), precision=lax.Precision.HIGHEST
    )
    owned = lax.psum_scatter(flat_partial, "rows", scatter_dimension=0, tiled=True)
    y_owned = owned.astype(jnp.bfloat16)
    y_group = lax.all_gather(y_owned, "rows", axis=0, tiled=True)
    column_term = lax.dot_general(
        local_matrix,
        y_group.astype(jnp.float32),
        (((0,), (0,)), ((), ())),
        precision=lax.Precision.HIGHEST,
    )
    z_share = lax.psum_scatter(column_term, "blk", scatter_dimension=0, tiled=True)
    return (y_owned[None], z_share[None])


def solution(mesh):
    placed = (
        P("rows", "blk", None),
        P("blk", "rows", None, None, None),
        P("blk", "rows", None),
        P("blk", "rows", None, None),
        P("blk", "rows"),
        P("blk", None),
    )
    devices = mesh.shape["blk"]
    fits = mesh.shape["rows"] == 2 and devices >= 8 and devices & (devices - 1) == 0
    return jax.shard_map(
        paired if fits else general,
        mesh=mesh,
        in_specs=placed,
        out_specs=(P("blk", "rows", None), P("rows", "blk", None)),
        check_vma=False,
    )
```

```python
import jax
import jax.numpy as jnp
from jax import lax
from jax.experimental import pallas as pl
from jax.experimental.pallas import tpu as pltpu
from jax.sharding import PartitionSpec as P


LANES = 128
NEXT = 2
SCALE_ROWS = 16
VMEM_BYTES = 24 << 20
PAIR_COST, TURNED_COST = 1 << 35, 1 << 31


def sides_of(chips):
    return tuple(
        [k for k in reversed(range(1, chips)) if k != NEXT and k.bit_count() % 2 == odd]
        for odd in (1, 0)
    )


def own_place(sides, shard):
    place = lax.axis_index("blk")
    core, chip = lax.rem(place, 2), lax.div(place, 2)

    def rows_at(offset, owner):
        which = lax.bitwise_xor(chip, offset)
        return pl.ds(pl.multiple_of(which * (2 * shard) + owner * shard, shard), shard)

    def rows_of(step, side, owner):
        return rows_at(jnp.where(side == 0, sides[0][step], sides[1][step]), owner)

    return core, rows_at, rows_of


def dot(a, b):
    return jnp.dot(a, b, preferred_element_type=jnp.float32)


def pair_kernel(q_own, q_far, pair):
    shard = q_own.shape[0]
    pair[0:shard, :] = q_own[...]
    pair[shard:, :] = q_far[...]


def front_kernel(rows, cols, count, owners, q_own, notes, q_copy):
    notes[...] = jnp.zeros_like(notes)
    notes[0:1, 0 : rows.shape[1]] = rows[...]
    notes[1:2, 0 : cols.shape[1]] = cols[...]
    notes[2:3, 0:1] = count[...]
    notes[3:4, 0 : owners.shape[1]] = owners[...]
    q_copy[...] = q_own[...]


def each_tile(notes, tiles):
    total, size = tiles.shape[:2]
    for t in range(total):
        tile = jnp.where(t < notes[2, 0], tiles[t], jnp.zeros_like(tiles[t]))
        yield tile, *(
            pl.ds(pl.multiple_of(notes[which, t] * size, size), size) for which in (0, 1)
        )


def coded_kernel(ours, given, sent):
    rows = ours.shape[0]
    x = ours[...] + given[...]
    top = jnp.max(jnp.abs(x), axis=0, keepdims=True)
    power = jnp.ceil(jnp.log2(jnp.maximum(top, 1e-30)))
    whole = jnp.clip(jnp.round(x * jnp.exp2(15.0 - power)), -32767.0, 32767.0)
    sent[0:rows, :] = whole.astype(jnp.int32).astype(jnp.int16)
    power = jnp.broadcast_to(power, (SCALE_ROWS, x.shape[1]))
    sent[rows:, :] = power.astype(jnp.int32).astype(jnp.int16)


def gather_kernel(*refs):
    *arrived, last, mine, theirs = refs
    shard = mine.shape[0]
    total = jnp.concatenate([last[0:shard, :], jnp.zeros_like(mine)], axis=0)
    for ref in arrived:
        x = ref[0 : 2 * shard, :].astype(jnp.int32).astype(jnp.float32)
        power = ref[2 * shard :, :].astype(jnp.int32).astype(jnp.float32)
        total = total + x * jnp.exp2(power[0:1, :] - 15.0)
    mine[...] = total[0:shard, :]
    theirs[...] = total[shard:, :]


def add_tiles(total, notes, tiles, q):
    for tile, rows, cols in each_tile(notes, tiles):
        total[rows, :] = total[rows, :] + dot(tile, q[cols, :])


def near_kernel(rounds, sides, *refs):
    block, beside, *refs = refs
    direct, relayed = refs[:rounds][::-1], refs[rounds : 2 * rounds][::-1]
    notes, tiles, y, q_far, q_near = refs[2 * rounds :]
    shard = block.shape[0] // 4
    core, rows_at, rows_of = own_place(sides, shard)

    def put(ref, rows, other):
        for part, at in enumerate((rows, other)):
            low = 2 * part * shard
            q_near[at, :] = ref[low : low + shard, :]
            q_far[at, :] = ref[low + shard : low + 2 * shard, :]

    for ref, offset in ((block, 0), (beside, NEXT)):
        put(ref, rows_at(offset, core), rows_at(offset, 1 - core))
    for step in range(rounds):
        for ref, side in ((direct[step], core), (relayed[step], 1 - core)):
            put(ref, rows_of(step, side, side), rows_of(step, side, 1 - side))
    y[...] = jnp.zeros_like(y)
    add_tiles(y, notes, tiles, q_near)


def turned_kernel(notes, tiles, high, low, a):
    a[...] = jnp.zeros_like(a)
    for tile, rows, cols in each_tile(notes, tiles):
        a[rows, cols] = a[rows, cols] + tile.astype(jnp.float32)
    turned = a[...].T
    high[...] = turned.astype(high.dtype)
    low[...] = (turned - high[...].astype(jnp.float32)).astype(low.dtype)


def product_kernel(rounds, sides, *refs):
    y_near, q_far, far_notes, far_tiles, high, low, y = refs[:7]
    keep, give = refs[7 : 8 + rounds], refs[8 + rounds : 9 + 2 * rounds]
    total, z = refs[9 + 2 * rounds :]
    total[...] = y_near[...]
    add_tiles(total, far_notes, far_tiles, q_far)
    y[...] = total[...].astype(y.dtype)
    z[...] = dot(high[...], y[...]) + dot(low[...], y[...])
    shard = keep[0].shape[0] // 2
    core, rows_at, rows_of = own_place(sides, shard)
    for step in range(rounds):
        for ref, side in ((keep[step], core), (give[step], 1 - core)):
            ref[0:shard, :] = z[rows_of(step, side, side), :]
            ref[shard : 2 * shard, :] = z[rows_of(step, side, 1 - side), :]
    for ref, side in ((keep[rounds], core), (give[rounds], 1 - core)):
        ref[0:shard, :] = z[rows_at(0, side), :]
        ref[shard : 2 * shard, :] = z[rows_at(NEXT, side), :]


def owned_kernel(group, y, notes, y_out):
    size = y.shape[0] // group
    mine = group // 2
    for k in range(group):
        slot = notes[3, k]

        @pl.when(lax.div(slot, mine) == lax.axis_index("rows"))
        def _():
            at = pl.multiple_of(lax.rem(slot, mine) * size, size)
            y_out[pl.ds(at, size), :] = y[k * size : (k + 1) * size, :]


def paired(q_panel, tiles, tile_rows, tile_cols, tile_count, owner_map):
    devices = lax.axis_size("blk")
    chips = devices // 2
    rounds = chips // 2 - 1
    sides = sides_of(chips)
    shard, rank = q_panel.shape[1:]
    stack = tiles[0, 0]
    total, size = stack.shape[:2]
    group = owner_map.shape[1]
    width = devices * shard
    height = group * size
    across = [(0, 1), (1, 0)]
    sibling = [(i, i ^ 1) for i in range(devices)]
    neighbour = [(i, i ^ (2 * NEXT)) for i in range(devices)]
    vmem = pl.BlockSpec(memory_space=pltpu.VMEM)

    def to_chips(step):
        return [
            (2 * m + c, 2 * (m ^ sides[c][step]) + c)
            for m in range(chips)
            for c in range(2)
        ]

    def call(body, name, outs, args, scratch=(), cost=0):
        return pl.pallas_call(
            body,
            out_shape=[jax.ShapeDtypeStruct(*out) for out in outs],
            in_specs=[vmem] * len(args),
            out_specs=[vmem] * len(outs),
            scratch_shapes=list(scratch),
            compiler_params=pltpu.CompilerParams(vmem_limit_bytes=VMEM_BYTES),
            cost_estimate=pl.CostEstimate(flops=cost, bytes_accessed=0, transcendentals=0)
            if cost
            else None,
            name=name,
        )(*args)

    q_own = q_panel[0]
    q_far = lax.ppermute(q_own, "rows", across)
    far_tiles = lax.ppermute(stack, "rows", across)
    notes, q_copy = call(
        front_kernel,
        "front",
        [((8, LANES), jnp.int32), (q_own.shape, q_own.dtype)],
        [
            tile_rows.reshape(1, total),
            tile_cols.reshape(1, total),
            tile_count,
            owner_map,
            q_own,
        ],
    )
    (pair,) = call(
        pair_kernel,
        "pair",
        [((2 * shard, rank), q_own.dtype)],
        [q_copy, q_far],
        cost=PAIR_COST,
    )
    block = jnp.concatenate([pair, lax.ppermute(pair, "blk", sibling)], axis=0)
    direct = [lax.ppermute(block, "blk", to_chips(step)) for step in range(rounds)]
    beside = lax.ppermute(block, "blk", neighbour)

    stack, notes, direct[0] = lax.optimization_barrier((stack, notes, direct[0]))
    turned = call(
        turned_kernel,
        "turned",
        [((width, height), stack.dtype)] * 2,
        [notes, stack],
        [pltpu.VMEM((height, width), jnp.float32)],
        cost=TURNED_COST,
    )
    far_notes = lax.ppermute(notes, "rows", across)
    relayed = [lax.ppermute(one, "blk", sibling) for one in direct]

    y_near, q_other = call(
        lambda *refs: near_kernel(rounds, sides, *refs),
        "near_products",
        [((height, rank), jnp.float32), ((width, rank), q_own.dtype)],
        [block, beside, *direct[::-1], *relayed[::-1], notes, stack],
        [pltpu.VMEM((width, rank), q_own.dtype)],
        cost=1,
    )
    y, *pieces = call(
        lambda *refs: product_kernel(rounds, sides, *refs),
        "products",
        [((height, rank), jnp.bfloat16)]
        + [((2 * shard, rank), jnp.float32)] * (2 * rounds + 2),
        [y_near, q_other, far_notes, far_tiles, *turned],
        [pltpu.VMEM((height, rank), jnp.float32), pltpu.VMEM((width, rank), jnp.float32)],
    )
    keep, give = pieces[: rounds + 1], pieces[rounds + 1 :]
    given = [lax.ppermute(one, "blk", sibling) for one in give]
    arrived = []
    for step in range(rounds):
        (sent,) = call(
            coded_kernel,
            "coded",
            [((2 * shard + SCALE_ROWS, rank), jnp.int16)],
            [keep[step], given[step]],
        )
        arrived.append(lax.ppermute(sent, "blk", to_chips(step)))
    last = keep[rounds] + given[rounds]
    z_beside = lax.ppermute(last[shard:], "blk", neighbour)
    y, arrived[0] = lax.optimization_barrier((y, arrived[0]))
    (y_owned,) = call(
        lambda *refs: owned_kernel(group, *refs),
        "owned",
        [((height // 2, rank), jnp.bfloat16)],
        [y, notes],
    )
    arrived[1], y_owned = lax.optimization_barrier((arrived[1], y_owned))
    z_mine, z_theirs = call(
        gather_kernel,
        "gathered",
        [((shard, rank), jnp.float32)] * 2,
        [*arrived, last],
    )
    z_share = z_mine + (lax.ppermute(z_theirs, "blk", sibling) + z_beside)
    return (y_owned[None], z_share[None])


def general(q_panel, tiles, tile_rows, tile_cols, tile_count, owner_map):
    panel_rows = q_panel.shape[1]
    tile_stack = tiles[0, 0]
    tile_total = tile_stack.shape[0]
    tile_size = tile_stack.shape[1]
    group_blocks = owner_map.shape[1]
    class_blocks = panel_rows * lax.axis_size("blk") // tile_size
    column_ids = tile_cols[0, 0, :, 0]
    active = jnp.arange(tile_total, dtype=jnp.int32) < tile_count[0, 0]
    slot_of_tile = owner_map[0][tile_rows[0, 0]]
    slot_hit = slot_of_tile[:, None] == jnp.arange(group_blocks, dtype=jnp.int32)[None, :]
    column_hit = column_ids[:, None] == jnp.arange(class_blocks, dtype=jnp.int32)[None, :]
    placing = (slot_hit[:, :, None] & column_hit[:, None, :] & active[:, None, None]).astype(
        tile_stack.dtype
    )
    local_matrix = jnp.einsum(
        "tsc,tik->sick", placing, tile_stack, preferred_element_type=jnp.float32
    )
    local_matrix = local_matrix.reshape(group_blocks * tile_size, class_blocks * tile_size)
    rows_in = lax.all_gather(q_panel, "blk", axis=1, tiled=True)[0]
    flat_partial = jnp.dot(
        local_matrix, rows_in.astype(jnp.float32), precision=lax.Precision.HIGHEST
    )
    owned = lax.psum_scatter(flat_partial, "rows", scatter_dimension=0, tiled=True)
    y_owned = owned.astype(jnp.bfloat16)
    y_group = lax.all_gather(y_owned, "rows", axis=0, tiled=True)
    column_term = lax.dot_general(
        local_matrix,
        y_group.astype(jnp.float32),
        (((0,), (0,)), ((), ())),
        precision=lax.Precision.HIGHEST,
    )
    z_share = lax.psum_scatter(column_term, "blk", scatter_dimension=0, tiled=True)
    return (y_owned[None], z_share[None])


def solution(mesh):
    placed = (
        P("rows", "blk", None),
        P("blk", "rows", None, None, None),
        P("blk", "rows", None),
        P("blk", "rows", None, None),
        P("blk", "rows"),
        P("blk", None),
    )
    devices = mesh.shape["blk"]
    fits = mesh.shape["rows"] == 2 and devices >= 8 and devices & (devices - 1) == 0
    return jax.shard_map(
        paired if fits else general,
        mesh=mesh,
        in_specs=placed,
        out_specs=(P("blk", "rows", None), P("rows", "blk", None)),
        check_vma=False,
    )
```
